128 devices in a mesh: dp: 32 (over z, y, core), tensor: 4 (over x).
Axes of the slice: x: 4, y: 4, z: 4, core: 2. Of those that a mesh axis runs over, the one named last changes fastest.
Arguments:
- hidden_in: bfloat16 [32768, 640], P(('dp', 'tensor')), may hold values from -6 to 6
- out_grad: bfloat16 [32768, 640], P(('dp', 'tensor')), may hold values from -6 to 6
- segment_ids: int32 [32768], P('dp'), may hold values from -1 to 1023, as said below
- gain_input: bfloat16 [640], P('dp'), may hold values from 0.25 to 1.75
- w_query: bfloat16 [640, 4, 256], P('dp', 'tensor'), may hold values from -0.25 to 0.25
- w_key: bfloat16 [640, 256], P('dp'), may hold values from -0.25 to 0.25
- w_value: bfloat16 [640, 256], P('dp'), may hold values from -0.25 to 0.25
- gain_query: bfloat16 [256], P('dp'), may hold values from 0.25 to 1.75
- gain_key: bfloat16 [256], P('dp'), may hold values from 0.25 to 1.75
- w_out: bfloat16 [640, 4, 256], P('dp', 'tensor'), may hold values from -0.1875 to 0.1875
- gain_attn: bfloat16 [640], P('dp'), may hold values from 0.25 to 1.75
- gain_ffin: bfloat16 [640], P('dp'), may hold values from 0.25 to 1.75
- w_gate: bfloat16 [640, 2048], P('dp', 'tensor'), may hold values from -0.25 to 0.25
- w_up: bfloat16 [640, 2048], P('dp', 'tensor'), may hold values from -0.25 to 0.25
- w_down: bfloat16 [640, 2048], P('dp', 'tensor'), may hold values from -0.125 to 0.125
- gain_ffout: bfloat16 [640], P('dp'), may hold values from 0.25 to 1.75
Outputs:
- layer_out: bfloat16 [32768, 640], P(('dp', 'tensor'))
- input_grad: float32 [32768, 640], P(('dp', 'tensor'))
- grad_gain_input: float32 [640], P('dp')
- grad_w_query: float32 [640, 4, 256], P('dp', 'tensor')
- grad_w_key: float32 [640, 256], P('dp')
- grad_w_value: float32 [640, 256], P('dp')
- grad_gain_query: float32 [256], P('dp')
- grad_gain_key: float32 [256], P('dp')
- grad_w_out: float32 [640, 4, 256], P('dp', 'tensor')
- grad_gain_attn: float32 [640], P('dp')
- grad_gain_ffin: float32 [640], P('dp')
- grad_w_gate: float32 [640, 2048], P('dp', 'tensor')
- grad_w_up: float32 [640, 2048], P('dp', 'tensor')
- grad_w_down: float32 [640, 2048], P('dp', 'tensor')
- grad_gain_ffout: float32 [640], P('dp')
The draws below stay inside these ranges and needn't reach their ends.
Inputs may be any that keep to these rules, and one draw needn't show every extreme that they name: `segment_ids`: each block of 1024 ids, in order, is one packed row: a live row's id is the index, within its block, of the first row of its document, so ids never fall over the live rows; a document is a run of equal ids of at most 1024 rows, and the live rows are followed by a tail of fewer than 256 entries of -1.
All inputs are finite; a program needn't handle non-finite values.
Results may differ from the reference program's by a relative error of at most 0.033.
Values may be sent and summed in bfloat16 or wider, within the bound.
No kernel may reach another device: no remote copies, remote signals or barrier semaphores. Data moves between devices by JAX's collectives and lax.ppermute only.
A program may use at most 128 MiB of HBM per device.

```python
import jax
import jax.numpy as jnp
from jax import lax

D = 640
HQ = 4
HD = 256
FF = 2048
WINDOW = 512
TOK_DEV = 256
GROUP = 1024
TOKENS = 32768


def draw_segment_ids(key, part):
    key = jax.random.fold_in(key, 7)
    groups_all = TOKENS // GROUP
    key_list = jax.random.split(key, 6)
    group_index = jnp.arange(groups_all, dtype=jnp.int32)
    pad_rows = jax.random.randint(key_list[0], (groups_all,), 0, TOK_DEV)
    full_group = jax.random.randint(key_list[1], (), 0, groups_all)
    short_group = (full_group + 1 + jax.random.randint(key_list[2], (), 0, groups_all - 2)) % groups_all
    last_group = (full_group + groups_all - 1) % groups_all
    pad_rows = jnp.where(group_index == full_group, 0, pad_rows)
    pad_rows = jnp.where(group_index == short_group, TOK_DEV - 1, pad_rows)
    pad_rows = jnp.where(group_index == last_group, 0, pad_rows)
    live_rows = GROUP - pad_rows
    prefix = jax.random.randint(key_list[3], (groups_all,), 0, TOK_DEV // 2 + 1)
    prefix = jnp.where(group_index == full_group, 0, prefix)
    span_low = 3 * TOK_DEV + 1 - prefix
    span_high = live_rows - prefix + 1
    span_rows = jax.random.randint(key_list[4], (groups_all,), span_low, span_high)
    span_rows = jnp.where(group_index == full_group, GROUP, span_rows)
    row_at = jnp.arange(GROUP, dtype=jnp.int32)[None, :]
    span_end = (prefix + span_rows)[:, None]
    cut_marks = (jax.random.randint(key_list[5], (groups_all, GROUP), 0, 64) == 0) & (row_at > span_end)
    rest_ids = 2 + jnp.cumsum(cut_marks.astype(jnp.int32), axis=1)
    labels = jnp.where(row_at < prefix[:, None], 0, jnp.where(row_at < span_end, 1, rest_ids))
    last_row = (group_index[:, None] == last_group) & (row_at == GROUP - 1)
    labels = jnp.where(last_row, 3 * GROUP + 5, labels)
    before = jnp.concatenate([jnp.full((groups_all, 1), -5, jnp.int32), labels[:, :-1]], axis=1)
    starts = lax.cummax(jnp.where(labels != before, row_at, 0), axis=1)
    doc_ids = jnp.where(row_at >= live_rows[:, None], -1, starts)
    return doc_ids.reshape(TOKENS).astype(jnp.int32)


def block_levels(own_key, extent, pieces, least, high):
    def one(axis_at, shards_of):
        heights = jax.random.uniform(jax.random.fold_in(jax.random.fold_in(own_key, 6), axis_at), (shards_of,), jnp.float32, least / len(pieces), high / len(pieces))
        return jnp.repeat(jnp.exp(heights), extent[axis_at] // shards_of).reshape((-1,) + (1,) * (len(extent) - axis_at - 1))

    gain = one(*pieces[0])
    for cut in pieces[1:]:
        gain = gain * one(*cut)
    return gain


def bell_draw(rng, shape, scale, bound, shards=(), kind=jnp.bfloat16):
    level = block_levels(rng, shape, shards, -0.22, 0.18) if shards else 1.0
    drawn = jax.random.normal(rng, shape, jnp.float32) * scale * level
    return jnp.minimum(jnp.maximum(drawn, -bound), bound).astype(kind)


def setup_inputs(seed: int = 0) -> dict:
    seeds = jax.random.split(jax.random.key(seed), 17)
    return {
        "hidden_in": bell_draw(seeds[0], (TOKENS, D), 1.0, 6.0, ((0, 128),)),
        "out_grad": bell_draw(seeds[1], (TOKENS, D), 1.0, 6.0, ((0, 128),)),
        "segment_ids": draw_segment_ids(jax.random.fold_in(seeds[16], 71), 0),
        "gain_input": jnp.clip(1.0 + 0.15 * jax.random.normal(seeds[3], (D,), jnp.float32), 0.25, 1.75).astype(jnp.bfloat16),
        "w_query": bell_draw(seeds[4], (D, HQ, HD), D ** -0.5, 0.25, ((0, 32), (1, 4))),
        "w_key": bell_draw(seeds[5], (D, HD), D ** -0.5, 0.25, ((0, 32),)),
        "w_value": bell_draw(seeds[6], (D, HD), D ** -0.5, 0.25, ((0, 32),)),
        "gain_query": jnp.clip(1.0 + 0.15 * jax.random.normal(seeds[7], (HD,), jnp.float32), 0.25, 1.75).astype(jnp.bfloat16),
        "gain_key": jnp.clip(1.0 + 0.15 * jax.random.normal(seeds[8], (HD,), jnp.float32), 0.25, 1.75).astype(jnp.bfloat16),
        "w_out": bell_draw(seeds[9], (D, HQ, HD), (HQ * HD) ** -0.5, 0.1875, ((0, 32), (1, 4))),
        "gain_attn": jnp.clip(1.0 + 0.15 * jax.random.normal(seeds[10], (D,), jnp.float32), 0.25, 1.75).astype(jnp.bfloat16),
        "gain_ffin": jnp.clip(1.0 + 0.15 * jax.random.normal(seeds[11], (D,), jnp.float32), 0.25, 1.75).astype(jnp.bfloat16),
        "w_gate": bell_draw(seeds[12], (D, FF), D ** -0.5, 0.25, ((0, 32), (1, 4))),
        "w_up": bell_draw(seeds[13], (D, FF), D ** -0.5, 0.25, ((0, 32), (1, 4))),
        "w_down": bell_draw(seeds[14], (D, FF), FF ** -0.5, 0.125, ((0, 32), (1, 4))),
        "gain_ffout": jnp.clip(1.0 + 0.15 * jax.random.normal(seeds[15], (D,), jnp.float32), 0.25, 1.75).astype(jnp.bfloat16),
    }


EPS = 1e-06
ROPE_BASE = 10000.0
NEGATIVE = -1e+30
EXACT_MODE = lax.Precision.HIGHEST

@jax.custom_vjp
def low(v):
    return lax.optimization_barrier(v.astype(jnp.bfloat16)).astype(jnp.float32)

@jax.custom_vjp
def low_back(v):
    return v

def low_keep(v):
    return (low(v), None)

def low_pass(kept, grad):
    return (grad,)

def back_keep(v):
    return (v, None)

def back_low(kept, grad):
    return (low(grad),)
low.defvjp(low_keep, low_pass)
low_back.defvjp(back_keep, back_low)

def norm_rows(values_in):
    return values_in * lax.rsqrt(lax.optimization_barrier(jnp.mean(values_in * values_in, axis=-1, keepdims=True)) + EPS)

def positions_of(segments):
    length_all = segments.shape[0]
    offsets = jnp.arange(length_all, dtype=jnp.int32)
    before = jnp.concatenate([jnp.full((1,), -3, jnp.int32), segments[:-1]], axis=0)
    starts = lax.cummax(jnp.where(segments != before, offsets, 0), axis=0)
    return offsets - starts

def rope_tables(positions, head_width):
    half_width = head_width // 2
    frequency = ROPE_BASE ** (-2.0 * jnp.arange(half_width, dtype=jnp.float32) / head_width)
    angles = positions.astype(jnp.float32)[:, None] * frequency[None, :]
    return (jnp.cos(angles), jnp.sin(angles))

def rotate(values_in, cosine_table, sine_table, direction):
    half_width = values_in.shape[-1] // 2
    first_half = values_in[..., :half_width]
    second = values_in[..., half_width:]
    cosine_rows = cosine_table[:, None, :]
    sine_rows = sine_table[:, None, :] * direction
    return jnp.concatenate([first_half * cosine_rows - second * sine_rows, second * cosine_rows + first_half * sine_rows], axis=-1)

def window_mask(block_at, padded_ids):
    offsets = jnp.arange(WINDOW, dtype=jnp.int32)
    query_at = block_at * WINDOW + offsets
    key_at = block_at * WINDOW - WINDOW + jnp.arange(2 * WINDOW, dtype=jnp.int32)
    query_ids = lax.dynamic_slice_in_dim(padded_ids, block_at * WINDOW + WINDOW, WINDOW, 0)
    key_ids = lax.dynamic_slice_in_dim(padded_ids, block_at * WINDOW, 2 * WINDOW, 0)
    same_doc = query_ids[:, None] == key_ids[None, :]
    behind = (key_at[None, :] <= query_at[:, None]) & (query_at[:, None] - key_at[None, :] < WINDOW)
    self_seen = (query_ids[:, None] >= 0) | (query_at[:, None] == key_at[None, :])
    return same_doc & behind & self_seen

def attention(query_rot, key_rot, value_low, segments):
    group_len = query_rot.shape[0]
    key_padded = jnp.concatenate([jnp.zeros((WINDOW, key_rot.shape[1]), jnp.float32), key_rot], axis=0)
    value_padded = jnp.concatenate([jnp.zeros((WINDOW, value_low.shape[1]), jnp.float32), value_low], axis=0)
    padded_ids = jnp.concatenate([jnp.full((WINDOW,), -2, jnp.int32), segments], axis=0)
    inverse = query_rot.shape[-1] ** (-0.5)

    def attend(block_at):
        start_row = block_at * WINDOW
        query_blk = lax.dynamic_slice_in_dim(query_rot, start_row, WINDOW, 0)
        key_blk = lax.dynamic_slice_in_dim(key_padded, start_row, 2 * WINDOW, 0)
        value_blk = lax.dynamic_slice_in_dim(value_padded, start_row, 2 * WINDOW, 0)
        scores = low_back(jnp.einsum('she,te->hst', query_blk, key_blk, precision=EXACT_MODE) * inverse)
        scores = jnp.where(window_mask(block_at, padded_ids)[None], scores, NEGATIVE)
        row_max = lax.optimization_barrier(jnp.max(scores, axis=-1, keepdims=True))
        exponent = jnp.exp(scores - row_max)
        attn_probs = low(exponent / lax.optimization_barrier(jnp.sum(exponent, axis=-1, keepdims=True)))
        return jnp.einsum('hst,te->she', attn_probs, value_blk, precision=EXACT_MODE)
    block_out = lax.map(jax.checkpoint(attend), jnp.arange(group_len // WINDOW, dtype=jnp.int32))
    return block_out.reshape(group_len, block_out.shape[2], block_out.shape[3])

def layer_group(resid_in, segments, gain_input, w_query, w_key, w_value, gain_query, gain_key, w_out, gain_attn, gain_ffin, w_gate, w_up, w_down, gain_ffout):
    rows_in = low(norm_rows(resid_in) * gain_input)
    query_raw = low_back(jnp.einsum('gd,dhe->ghe', rows_in, w_query, precision=EXACT_MODE))
    key_raw = low_back(jnp.dot(rows_in, w_key, precision=EXACT_MODE))
    value_low = low(low_back(jnp.dot(rows_in, w_value, precision=EXACT_MODE)))
    cosine_table, sine_table = rope_tables(positions_of(segments), key_raw.shape[-1])
    query_rot = low(rotate(norm_rows(query_raw) * gain_query, cosine_table, sine_table, 1.0))
    key_rot = low(rotate((norm_rows(key_raw) * gain_key)[:, None, :], cosine_table, sine_table, 1.0)[:, 0, :])
    attended = low(low_back(attention(query_rot, key_rot, value_low, segments)))
    attn_sum = low_back(jnp.einsum('ghe,dhe->gd', attended, w_out, precision=EXACT_MODE))
    resid_mid = resid_in + norm_rows(attn_sum) * gain_attn
    rows_mid = low(norm_rows(resid_mid) * gain_ffin)
    gate_pre = low_back(jnp.dot(rows_mid, w_gate, precision=EXACT_MODE))
    up_pre = low_back(jnp.dot(rows_mid, w_up, precision=EXACT_MODE))
    hidden_low = low(jax.nn.gelu(gate_pre, approximate=True) * up_pre)
    ff_sum = low_back(jnp.einsum('gf,df->gd', hidden_low, w_down, precision=EXACT_MODE))
    return resid_mid + norm_rows(ff_sum) * gain_ffout

def reference(hidden_in, out_grad, segment_ids, gain_input, w_query, w_key, w_value, gain_query, gain_key, w_out, gain_attn, gain_ffin, w_gate, w_up, w_down, gain_ffout):
    params_list = [each_param.astype(jnp.float32) for each_param in (gain_input, w_query, w_key, w_value, gain_query, gain_key, w_out, gain_attn, gain_ffin, w_gate, w_up, w_down, gain_ffout)]
    resid_in = hidden_in.astype(jnp.float32)

    def whole(resid_all, *weights_all):
        rows_grouped = resid_all.reshape(TOKENS // GROUP, GROUP, D)
        ids_grouped = segment_ids.reshape(TOKENS // GROUP, GROUP)

        def one_group(pair_in):
            return layer_group(pair_in[0], pair_in[1], *weights_all)
        return lax.map(jax.checkpoint(one_group), (rows_grouped, ids_grouped)).reshape(TOKENS, D)
    layer_all, back_fn = jax.vjp(whole, resid_in, *params_list)
    grads = back_fn(out_grad.astype(jnp.float32))
    return (layer_all.astype(jnp.bfloat16), grads[0], grads[1], grads[2], grads[3], grads[4], grads[5], grads[6], grads[7], grads[8], grads[9], grads[10], grads[11], grads[12], grads[13])
```

```python
import jax
import jax.numpy as jnp
from jax import lax
from jax.sharding import Mesh, PartitionSpec as P

WINDOW = 512
EPS = 1e-06
ROPE_BASE = 10000.0
NEGATIVE = -1e30
ZS, YS, CS, XS = 4, 4, 2, 4
CHIP = ("z", "y", "x")
EVERY = ("z", "y", "core", "x")
DPS = 32
OWN = 20
PAD = 24
DM = 640
DP = DPS * PAD
ROWS = 256
HQ = 4
HD = 256
FFN = 2048
BF = jnp.bfloat16
F32 = jnp.float32


def mean_rows(values_in):
    return jnp.sum(values_in, axis=-1, keepdims=True) * (1.0 / DM)


def norm_wide(values_in):
    return values_in * lax.rsqrt(mean_rows(values_in * values_in) + EPS)


def norm_back_wide(values_in, upstream):
    inverse = lax.rsqrt(mean_rows(values_in * values_in) + EPS)
    normed = values_in * inverse
    return inverse * (upstream - normed * mean_rows(upstream * normed))


def norm_rows(values_in):
    return values_in * lax.rsqrt(jnp.mean(values_in * values_in, axis=-1, keepdims=True) + EPS)


def norm_back(values_in, upstream):
    inverse = lax.rsqrt(jnp.mean(values_in * values_in, axis=-1, keepdims=True) + EPS)
    normed = values_in * inverse
    return inverse * (upstream - normed * jnp.mean(upstream * normed, axis=-1, keepdims=True))


def gelu_tanh(values_in):
    return jax.nn.gelu(values_in, approximate=True)


def rotate(values_in, cosine_rows, sine_rows):
    half_width = values_in.shape[-1] // 2
    first_half = values_in[..., :half_width]
    second = values_in[..., half_width:]
    return jnp.concatenate(
        [
            first_half * cosine_rows - second * sine_rows,
            second * cosine_rows + first_half * sine_rows,
        ],
        axis=-1,
    )


def dot(lhs, rhs, lhs_dim, rhs_dim):
    return lax.dot_general(
        lhs, rhs, (((lhs_dim,), (rhs_dim,)), ((), ())), preferred_element_type=F32
    )


def spread_matrix():
    row = lax.broadcasted_iota(jnp.int32, (DM, DP), 0)
    col = lax.broadcasted_iota(jnp.int32, (DM, DP), 1)
    block, inner = col // PAD, col % PAD
    core, chip = block // 16, block % 16
    return ((inner < OWN) & (row == (chip * CS + core) * OWN + inner)).astype(BF)


def per_device(
    hidden_in,
    out_grad,
    segment_ids,
    gain_input,
    w_query,
    w_key,
    w_value,
    gain_query,
    gain_key,
    w_out,
    gain_attn,
    gain_ffin,
    w_gate,
    w_up,
    w_down,
    gain_ffout,
):
    at = lax.axis_index("x")
    core = lax.axis_index("core")

    kv_own = jnp.concatenate([w_key, w_value], axis=1)
    kv_own = lax.dynamic_slice_in_dim(kv_own, at * 128, 128, 1)
    gains_own = jnp.stack(
        [
            gain_input,
            gain_attn,
            gain_ffin,
            gain_ffout,
            jnp.pad(gain_query, (0, OWN - 8)),
            jnp.pad(gain_key, (0, OWN - 8)),
        ],
        axis=1,
    )
    gains_own = jnp.pad(gains_own, ((0, 0), (0, 122)))
    packed = jnp.concatenate(
        [w_query[:, 0], w_out[:, 0], w_gate, w_up, w_down, kv_own, gains_own], axis=1
    )
    packed = jnp.pad(packed, ((0, PAD - OWN), (0, 0)))
    width = packed.shape[1]
    gathered = lax.all_gather(packed, EVERY, axis=0, tiled=False)
    gathered = gathered.reshape(16, CS, XS, PAD, width)

    before_one = lax.ppermute(hidden_in, "x", [(i, i + 1) for i in range(XS - 1)])
    before_two = lax.ppermute(hidden_in, "x", [(i, i + 2) for i in range(XS - 2)])
    rows_low = jnp.concatenate([before_two, before_one, hidden_in], axis=0)
    spread = spread_matrix()
    resid_all = dot(rows_low, spread, 1, 0)
    upstream = dot(out_grad, spread, 1, 0)
    normed_all = norm_wide(resid_all)
    resid_in = resid_all[2 * ROWS :]

    offsets = jnp.arange(segment_ids.shape[0], dtype=jnp.int32)
    live = segment_ids >= 0
    tail_start = jnp.sum(live.astype(jnp.int32))
    positions = offsets - jnp.where(live, segment_ids, tail_start)
    positions = jnp.concatenate([jnp.zeros((2 * ROWS,), jnp.int32), positions], axis=0)
    positions = lax.dynamic_slice_in_dim(positions, at * ROWS, 3 * ROWS, 0)
    half = HD // 2
    frequency = ROPE_BASE ** (-2.0 * jnp.arange(half, dtype=F32) / HD)
    angles = positions.astype(F32)[:, None] * frequency[None, :]
    cosine_all, sine_all = jnp.cos(angles), jnp.sin(angles)
    cosine_own, sine_own = cosine_all[2 * ROWS :, None], sine_all[2 * ROWS :, None]
    ids = jnp.concatenate([jnp.full((2 * ROWS,), -2, jnp.int32), segment_ids], axis=0)
    key_ids = lax.dynamic_slice_in_dim(ids, at * ROWS, 3 * ROWS, 0)
    query_ids = key_ids[2 * ROWS :]
    row_at = lax.broadcasted_iota(jnp.int32, (ROWS, 3 * ROWS), 0)
    col_at = lax.broadcasted_iota(jnp.int32, (ROWS, 3 * ROWS), 1)
    gap = row_at + 2 * ROWS - col_at
    visible = (
        (query_ids[:, None] == key_ids[None, :])
        & (gap >= 0)
        & (gap < WINDOW)
        & ((query_ids[:, None] >= 0) | (gap == 0))
    )

    def whole(first, size):
        part = gathered[..., first : first + size]
        return part.transpose(1, 0, 3, 2, 4).reshape(DP, XS * size)

    full_wq = whole(0, 256)
    full_wo = whole(256, 256)
    full_wg = whole(512, 512)
    full_wu = whole(1024, 512)
    full_wd = whole(1536, 512)
    full_wkv = whole(2048, 128)
    gain_cols = gathered[:, :, 0, :, 2176:2184].transpose(1, 0, 2, 3)
    model_gains = gain_cols[..., :4].reshape(DP, 4).T.astype(F32)
    input_gains, attn_gains, ffin_gains, ffout_gains = (model_gains[i : i + 1] for i in range(4))
    head_gains = gain_cols[..., :8, 4:6].transpose(3, 1, 0, 2).reshape(2, HD).astype(F32)
    query_gains, key_gains = head_gains[0], head_gains[1]

    rows_all = (normed_all * input_gains).astype(BF)
    rows_own = rows_all[2 * ROWS :]
    query_raw = dot(rows_own, full_wq, 1, 0).reshape(ROWS, HQ, HD)
    kv_raw = dot(rows_all, full_wkv, 1, 0)
    key_raw = kv_raw[:, :HD]
    value_low = kv_raw[:, HD:].astype(BF)
    query_norm = norm_rows(query_raw)
    key_norm = norm_rows(key_raw)
    query_rot = rotate(query_norm * query_gains, cosine_own, sine_own).astype(BF)
    key_rot = rotate(key_norm * key_gains, cosine_all, sine_all).astype(BF)

    inverse = HD**-0.5
    scores = jnp.einsum("she,te->hst", query_rot, key_rot, preferred_element_type=F32) * inverse
    scores = jnp.where(visible[None], scores, NEGATIVE)
    row_max = jnp.max(scores, axis=-1, keepdims=True)
    exponent = jnp.exp(scores - row_max)
    totals = jnp.sum(exponent, axis=-1, keepdims=True)
    probs = exponent / totals
    probs_low = probs.astype(BF)
    attended = jnp.einsum("hst,te->she", probs_low, value_low, preferred_element_type=F32)
    attended = attended.reshape(ROWS, HQ * HD).astype(BF)
    attn_sum = dot(attended, full_wo, 1, 1)
    attn_normed = norm_wide(attn_sum)
    resid_mid = resid_in + attn_normed * attn_gains
    normed_mid = norm_wide(resid_mid)
    rows_mid = (normed_mid * ffin_gains).astype(BF)
    gate_pre = dot(rows_mid, full_wg, 1, 0)
    up_pre = dot(rows_mid, full_wu, 1, 0)
    gate_act, gelu_back = jax.vjp(gelu_tanh, gate_pre)
    hidden_low = (gate_act * up_pre).astype(BF)
    ff_sum = dot(hidden_low, full_wd, 1, 1)
    ff_normed = norm_wide(ff_sum)
    layer_out = (resid_mid + ff_normed * ffout_gains).astype(BF)
    layer_out = dot(layer_out, spread, 1, 1).astype(BF)

    grad_gout = jnp.sum(upstream * ff_normed, axis=0)
    grad_ff = norm_back_wide(ff_sum, upstream * ffout_gains).astype(BF)
    grad_hidden = dot(grad_ff, full_wd, 1, 0)
    grad_wd = dot(grad_ff, hidden_low, 0, 0).astype(BF)
    grad_gate = gelu_back(grad_hidden * up_pre)[0].astype(BF)
    grad_up = (grad_hidden * gate_act).astype(BF)
    grad_wg = dot(rows_mid, grad_gate, 0, 0).astype(BF)
    grad_wu = dot(rows_mid, grad_up, 0, 0).astype(BF)
    grad_mid = dot(grad_gate, full_wg, 1, 1) + dot(grad_up, full_wu, 1, 1)
    grad_gfin = jnp.sum(grad_mid * normed_mid, axis=0)
    grad_resid = upstream + norm_back_wide(resid_mid, grad_mid * ffin_gains)
    grad_gattn = jnp.sum(grad_resid * attn_normed, axis=0)
    grad_attn = norm_back_wide(attn_sum, grad_resid * attn_gains).astype(BF)
    grad_wo = dot(grad_attn, attended, 0, 0).astype(BF)
    grad_attended = dot(grad_attn, full_wo, 1, 0).astype(BF).reshape(ROWS, HQ, HD)

    grad_value = jnp.einsum("hst,she->te", probs_low, grad_attended, preferred_element_type=F32)
    grad_probs = jnp.einsum("she,te->hst", grad_attended, value_low, preferred_element_type=F32)
    grad_scores = (
        probs * (grad_probs - jnp.sum(probs * grad_probs, axis=-1, keepdims=True))
    ).astype(BF)
    grad_query = (
        jnp.einsum("hst,te->she", grad_scores, key_rot, preferred_element_type=F32) * inverse
    )
    grad_key = (
        jnp.einsum("hst,she->te", grad_scores, query_rot, preferred_element_type=F32) * inverse
    )
    grad_query_norm = rotate(grad_query, cosine_own, -sine_own)
    grad_gq = jnp.sum(grad_query_norm * query_norm, axis=(0, 1))
    grad_query_raw = norm_back(query_raw, grad_query_norm * query_gains).astype(BF)
    grad_query_raw = grad_query_raw.reshape(ROWS, HQ * HD)
    grad_key_norm = rotate(grad_key, cosine_all, -sine_all)
    grad_gk = jnp.sum(grad_key_norm * key_norm, axis=0)
    grad_key_raw = norm_back(key_raw, grad_key_norm * key_gains)
    grad_kv = jnp.concatenate([grad_key_raw, grad_value], axis=1).astype(BF)
    grad_wq = dot(rows_own, grad_query_raw, 0, 0).astype(BF)
    grad_wkv = dot(rows_all, grad_kv, 0, 0).astype(BF)

    query_part = dot(grad_query_raw, full_wq, 1, 1)
    kv_part = dot(grad_kv, full_wkv, 1, 1)
    normed_in = normed_all[2 * ROWS :]
    grad_gin = jnp.sum(query_part * normed_in, axis=0) + jnp.sum(kv_part * normed_all, axis=0)

    from_one = lax.ppermute(
        grad_kv[ROWS : 2 * ROWS], "x", [(i + 1, i) for i in range(XS - 1)]
    )
    from_two = lax.ppermute(grad_kv[:ROWS], "x", [(i + 2, i) for i in range(XS - 2)])
    grad_kv_own = (
        grad_kv[2 * ROWS :].astype(F32) + from_one.astype(F32) + from_two.astype(F32)
    ).astype(BF)
    grad_in = query_part + dot(grad_kv_own, full_wkv, 1, 1)
    input_grad = grad_resid + norm_back_wide(resid_in, grad_in * input_gains)
    grad_top = input_grad.astype(BF)
    grad_rest = (input_grad - grad_top.astype(F32)).astype(BF)
    input_grad = dot(grad_top, spread, 1, 1) + dot(grad_rest, spread, 1, 1)

    model_part = jnp.stack([grad_gin, grad_gattn, grad_gfin, grad_gout], axis=1)
    head_part = jnp.stack([grad_gq, grad_gk], axis=1).reshape(16, CS, 8, 2)
    head_part = jnp.pad(head_part.transpose(1, 0, 2, 3), ((0, 0), (0, 0), (0, PAD - 8), (0, 0)))
    gains_part = jnp.concatenate([model_part, head_part.reshape(DP, 2)], axis=1)
    gains_part = jnp.pad(gains_part, ((0, 0), (0, 122))).astype(BF)

    def pieces(grad, size):
        return grad.reshape(CS, 16, PAD, XS, size).transpose(0, 1, 3, 2, 4)

    def same(grad):
        size = grad.shape[1]
        return jnp.broadcast_to(
            grad.reshape(CS, 16, 1, PAD, size), (CS, 16, XS, PAD, size)
        )

    grads = jnp.concatenate(
        [
            pieces(grad_wq, 256),
            pieces(grad_wo, 256),
            pieces(grad_wg, 512),
            pieces(grad_wu, 512),
            pieces(grad_wd, 512),
            same(grad_wkv),
            same(gains_part),
        ],
        axis=-1,
    )
    away = lax.dynamic_index_in_dim(grads, 1 - core, 0, keepdims=False)
    kept = lax.dynamic_index_in_dim(grads, core, 0, keepdims=False)
    arrived = lax.ppermute(away, "core", [(0, 1), (1, 0)])
    chip_sum = (kept.astype(F32) + arrived.astype(F32)).astype(BF)
    chip_sum = chip_sum.reshape(64, PAD, chip_sum.shape[-1])
    parts = lax.all_to_all(chip_sum, CHIP, 0, 0, tiled=True)
    total = jnp.sum(parts.astype(F32), axis=0)[:OWN]
    gains_total = total[:, 2560:]
    return (
        layer_out,
        input_grad,
        gains_total[:, 0],
        total[:, None, 0:256],
        total[:, 2048:2304],
        total[:, 2304:2560],
        gains_total[:8, 4],
        gains_total[:8, 5],
        total[:, None, 256:512],
        gains_total[:, 1],
        gains_total[:, 2],
        total[:, 512:1024],
        total[:, 1024:1536],
        total[:, 1536:2048],
        gains_total[:, 3],
    )


def solution(mesh):
    fine = Mesh(mesh.devices.reshape(ZS, YS, CS, XS), EVERY)
    dp = ("z", "y", "core")
    in_specs = (
        P(EVERY, None),
        P(EVERY, None),
        P(dp),
        P(dp),
        P(dp, "x", None),
        P(dp, None),
        P(dp, None),
        P(dp),
        P(dp),
        P(dp, "x", None),
        P(dp),
        P(dp),
        P(dp, "x"),
        P(dp, "x"),
        P(dp, "x"),
        P(dp),
    )
    out_specs = (
        P(EVERY, None),
        P(EVERY, None),
        P(dp),
        P(dp, "x", None),
        P(dp, None),
        P(dp, None),
        P(dp),
        P(dp),
        P(dp, "x", None),
        P(dp),
        P(dp),
        P(dp, "x"),
        P(dp, "x"),
        P(dp, "x"),
        P(dp),
    )
    return jax.shard_map(
        per_device, mesh=fine, in_specs=in_specs, out_specs=out_specs, check_vma=False
    )
```

```python
import jax
import jax.numpy as jnp
from jax import lax
from jax.experimental import pallas as pl
from jax.experimental.pallas import tpu as pltpu
from jax.sharding import Mesh, PartitionSpec as P

WINDOW = 512
EPS = 1e-06
ROPE_BASE = 10000.0
NEGATIVE = -1e30
ZS, YS, CS, XS = 4, 4, 2, 4
CHIP = ("z", "y", "x")
EVERY = ("z", "y", "core", "x")
DPS = 32
OWN = 20
PAD = 24
DM = 640
DP = DPS * PAD
ROWS = 256
KEYS = 3 * ROWS
HQ = 4
HD = 256
HALF = HD // 2
ATT = 768
FFC = 1536
SCALE = HD**-0.5
GELU_C = 0.7978845608028654
GELU_A = 0.044715
BF = jnp.bfloat16
F32 = jnp.float32
VMEM = 60 * 2**20


def norm_of(values_in, width):
    inverse = lax.rsqrt(
        jnp.sum(values_in * values_in, axis=-1, keepdims=True) * (1.0 / width) + EPS
    )
    return values_in * inverse, inverse


def norm_back(normed, inverse, upstream, width):
    mean = jnp.sum(upstream * normed, axis=-1, keepdims=True) * (1.0 / width)
    return inverse * (upstream - normed * mean)


def rotate(values_in, cosine, sine):
    first, second = values_in[:, :HALF], values_in[:, HALF:]
    return jnp.concatenate(
        [first * cosine - second * sine, second * cosine + first * sine], axis=1
    )


def dot(lhs, rhs, lhs_dim, rhs_dim):
    return lax.dot_general(
        lhs, rhs, (((lhs_dim,), (rhs_dim,)), ((), ())), preferred_element_type=F32
    )


def spread_matrix():
    row = lax.broadcasted_iota(jnp.int32, (DM, DP), 0)
    col = lax.broadcasted_iota(jnp.int32, (DM, DP), 1)
    return ((col % PAD < OWN) & (row == (col // PAD) * OWN + col % PAD)).astype(BF)


def head_matrix(step):
    row = lax.broadcasted_iota(jnp.int32, (DPS * step, HD), 0)
    col = lax.broadcasted_iota(jnp.int32, (DPS * step, HD), 1)
    return ((row // step == col // 8) & (row % step == col % 8)).astype(BF)


def fetch(gathered, held, sems, first, size):
    copies = [
        pltpu.make_async_copy(gathered.at[:, x, :, first : first + size], held.at[x], sems.at[x])
        for x in range(XS)
    ]
    for copy in copies:
        copy.start()
    return copies


def cut(held, x, first, size):
    return held[x, :, :, first : first + size].reshape(DP, size)


def kv_weights(watt):
    return jnp.concatenate([cut(watt, x, 512, 128) for x in range(XS)], axis=1)


def pack_kernel(wq_ref, wo_ref, wg_ref, wu_ref, wd_ref, wk_ref, wv_ref, gains_ref, at_ref, out):
    out[...] = jnp.zeros(out.shape, BF)
    out[0:OWN, 0:256] = wq_ref[:, 0, :]
    out[0:OWN, 256:512] = wo_ref[:, 0, :]
    at = at_ref[0]
    kv = jnp.where(
        jnp.broadcast_to(at, (OWN, 256)) < 2, wk_ref[...].astype(F32), wv_ref[...].astype(F32)
    )
    kv = jnp.where(jnp.broadcast_to(at % 2, (OWN, 128)) == 0, kv[:, :128], kv[:, 128:])
    out[0:OWN, 512:640] = kv.astype(BF)
    out[:, 640:768] = gains_ref[...].T[:PAD].astype(BF)
    out[0:OWN, 768:1280] = wg_ref[...]
    out[0:OWN, 1280:1792] = wu_ref[...]
    out[0:OWN, 1792:2304] = wd_ref[...]


def attend_kernel(
    gathered, normed_ref, cosine_ref, sine_ref, bias_ref, heads_ref,
    gains_out, rows_out, qraw_out, kvraw_out, q_out, k_out, v_out, probs_out, mixed_out, attn_out,
    watt, sems,
):
    for copy in fetch(gathered, watt, sems, 0, ATT):
        copy.wait()
    gains = cut(watt, 0, 640, 128).astype(F32).T
    gains_out[0:8] = gains[0:8]
    head_gains = dot(gains.astype(BF), heads_ref[...], 1, 0)
    gains_out[8:16] = jnp.concatenate([head_gains[0:8]] * 3, axis=1)
    query_gains, key_gains = head_gains[4:5], head_gains[5:6]
    rows = (normed_ref[...] * gains[0:1]).astype(BF)
    rows_out[...] = rows
    kv_raw = dot(rows, kv_weights(watt), 1, 0)
    kvraw_out[...] = kv_raw
    key_norm, _ = norm_of(kv_raw[:, :HD], HD)
    key = rotate(key_norm * key_gains, cosine_ref[...], sine_ref[...]).astype(BF)
    value = kv_raw[:, HD:].astype(BF)
    k_out[...] = key
    v_out[...] = value
    rows_own = rows[2 * ROWS :]
    cosine, sine = cosine_ref[2 * ROWS :], sine_ref[2 * ROWS :]
    attn = jnp.zeros((ROWS, DP), F32)
    for head in range(HQ):
        at = slice(head * HD, (head + 1) * HD)
        query_raw = dot(rows_own, cut(watt, head, 0, 256), 1, 0)
        qraw_out[:, at] = query_raw
        query_norm, _ = norm_of(query_raw, HD)
        query = rotate(query_norm * query_gains, cosine, sine).astype(BF)
        q_out[:, at] = query
        scores = dot(query, key, 1, 1) * SCALE + bias_ref[...]
        exponent = jnp.exp(scores - jnp.max(scores, axis=-1, keepdims=True))
        probs = exponent * (1.0 / jnp.sum(exponent, axis=-1, keepdims=True))
        probs_out[head] = probs
        mixed = dot(probs.astype(BF), value, 1, 0).astype(BF)
        mixed_out[:, at] = mixed
        attn = attn + dot(mixed, cut(watt, head, 256, 256), 1, 1)
    attn_out[...] = attn


def feed_kernel(
    core_ref, gathered, attn_ref, resid_ref, up_ref, gains_ref, spread_ref,
    layer_out, dres_out, dattn_out, away_out, sums_out, z_s, dg_s, du_s, rows_t_out, ff_t_out,
    gate_s, upp_s, wff, sems,
):
    copies = fetch(gathered, wff, sems, ATT, FFC)
    attn_gains, ffin_gains, ffout_gains = gains_ref[1:2], gains_ref[2:3], gains_ref[3:4]
    spread = spread_ref[...]
    upstream = up_ref[...]
    attn_normed, attn_inv = norm_of(attn_ref[...], DM)
    mid = resid_ref[...] + attn_normed * attn_gains
    mid_normed, mid_inv = norm_of(mid, DM)
    rows = (mid_normed * ffin_gains).astype(BF)
    ff_sum = jnp.zeros((ROWS, DP), F32)
    for x in range(XS):
        at = slice(x * 512, (x + 1) * 512)
        copies[x].wait()
        gate = dot(rows, cut(wff, x, 0, 512), 1, 0)
        up = dot(rows, cut(wff, x, 512, 512), 1, 0)
        gate_s[:, at] = gate
        upp_s[:, at] = up
        act = 0.5 * gate * (1.0 + jnp.tanh(GELU_C * (gate + GELU_A * gate * gate * gate)))
        hidden = (act * up).astype(BF)
        z_s[:, at] = hidden
        ff_sum = ff_sum + dot(hidden, cut(wff, x, 1024, 512), 1, 1)
    ff_normed, ff_inv = norm_of(ff_sum, DM)
    layer = (mid + ff_normed * ffout_gains).astype(BF)
    layer_out[...] = dot(layer, spread, 1, 1).astype(BF)
    grad_gout = jnp.sum(upstream * ff_normed, axis=0, keepdims=True)
    grad_ff = norm_back(ff_normed, ff_inv, upstream * ffout_gains, DM).astype(BF)
    grad_mid = jnp.zeros((ROWS, DP), F32)
    for x in range(XS):
        at = slice(x * 512, (x + 1) * 512)
        grad_hidden = dot(grad_ff, cut(wff, x, 1024, 512), 1, 0)
        gate, up = gate_s[:, at], upp_s[:, at]
        curve = jnp.tanh(GELU_C * (gate + GELU_A * gate * gate * gate))
        slope = 0.5 * (1.0 + curve) + 0.5 * gate * (1.0 - curve * curve) * (
            GELU_C * (1.0 + 3.0 * GELU_A * gate * gate)
        )
        grad_gate = (grad_hidden * up * slope).astype(BF)
        grad_up = (grad_hidden * (0.5 * gate * (1.0 + curve))).astype(BF)
        dg_s[:, at] = grad_gate
        du_s[:, at] = grad_up
        grad_mid = grad_mid + dot(grad_gate, cut(wff, x, 0, 512), 1, 1)
        grad_mid = grad_mid + dot(grad_up, cut(wff, x, 512, 512), 1, 1)
    grad_gfin = jnp.sum(grad_mid * mid_normed, axis=0, keepdims=True)
    grad_resid = upstream + norm_back(mid_normed, mid_inv, grad_mid * ffin_gains, DM)
    dres_out[...] = grad_resid
    grad_gattn = jnp.sum(grad_resid * attn_normed, axis=0, keepdims=True)
    dattn_out[...] = norm_back(attn_normed, attn_inv, grad_resid * attn_gains, DM).astype(BF)
    zero = jnp.zeros((1, DP), F32)
    sums_out[...] = jnp.concatenate(
        [zero, grad_gattn, grad_gfin, grad_gout, zero, zero, zero, zero], axis=0
    )
    rows_t = dot(spread, rows, 1, 1).astype(BF)
    ff_t = dot(spread, grad_ff, 1, 1).astype(BF)
    rows_t_out[...] = rows_t
    ff_t_out[...] = ff_t
    feed_half(1 - core_ref[0], away_out, rows_t, ff_t, z_s, dg_s, du_s)


def feed_half(half, out, rows_t, ff_t, z_ref, dg_ref, du_ref):
    for x in range(XS):
        cols = pl.ds(pl.multiple_of(x * 512 + half * 256, 256), 256)
        for part, (lhs, rhs) in enumerate(((rows_t, dg_ref), (rows_t, du_ref), (ff_t, z_ref))):
            grad = dot(lhs, rhs[:, cols], 1, 0).reshape(16, 40, 256).astype(BF)
            out[:, x, :, part * 256 : (part + 1) * 256] = grad


def feed_keep_kernel(core_ref, z_ref, dg_ref, du_ref, rows_t_ref, ff_t_ref, keep_out):
    feed_half(core_ref[0], keep_out, rows_t_ref[...], ff_t_ref[...], z_ref, dg_ref, du_ref)


def attend_back_kernel(
    core_ref, gathered, dattn_ref, rows_ref, normed_ref, qraw_ref, kvraw_ref, q_ref, k_ref, v_ref,
    probs_ref, mixed_ref, cosine_ref, sine_ref, gains_ref, sums_ref, spread_ref, heads_ref,
    keep_out, away_out, dkv_out, part_out, wq_s, wo_s, wkv_s, watt, sems,
):
    copies = fetch(gathered, watt, sems, 0, ATT)
    spread = spread_ref[...]
    query_gains, key_gains = gains_ref[12:13, :HD], gains_ref[13:14, :HD]
    grad_attn = dattn_ref[...]
    attn_t = dot(spread, grad_attn, 1, 1).astype(BF)
    rows_t = dot(spread, rows_ref[...], 1, 1).astype(BF)
    rows_own_t = rows_t[:, 2 * ROWS :]
    key, value = k_ref[...], v_ref[...]
    cosine, sine = cosine_ref[2 * ROWS :], sine_ref[2 * ROWS :]
    for copy in copies:
        copy.wait()
    grad_key = jnp.zeros((KEYS, HD), F32)
    grad_value = jnp.zeros((KEYS, HD), F32)
    part = jnp.zeros((ROWS, DP), F32)
    grad_gq = jnp.zeros((1, HD), F32)
    for head in range(HQ):
        at = slice(head * HD, (head + 1) * HD)
        grad_mixed = dot(grad_attn, cut(watt, head, 256, 256), 1, 0).astype(BF)
        wo_s[:, at] = dot(attn_t, mixed_ref[:, at], 1, 0).astype(BF)
        probs = probs_ref[head]
        grad_value = grad_value + dot(probs.astype(BF), grad_mixed, 0, 0)
        grad_probs = dot(grad_mixed, value, 1, 1)
        grad_scores = (
            probs * (grad_probs - jnp.sum(probs * grad_probs, axis=-1, keepdims=True))
        ).astype(BF)
        grad_query = dot(grad_scores, key, 1, 0) * SCALE
        grad_key = grad_key + dot(grad_scores, q_ref[:, at], 0, 0)
        query_norm, query_inv = norm_of(qraw_ref[:, at], HD)
        grad_query = rotate(grad_query, cosine, -sine)
        grad_gq = grad_gq + jnp.sum(grad_query * query_norm, axis=0, keepdims=True)
        grad_raw = norm_back(query_norm, query_inv, grad_query * query_gains, HD).astype(BF)
        part = part + dot(grad_raw, cut(watt, head, 0, 256), 1, 1)
        wq_s[:, at] = dot(rows_own_t, grad_raw, 1, 0).astype(BF)
    part_out[...] = part
    key_norm, key_inv = norm_of(kvraw_ref[:, :HD], HD)
    grad_key = rotate(grad_key * SCALE, cosine_ref[...], -sine_ref[...])
    grad_gk = jnp.sum(grad_key * key_norm, axis=0, keepdims=True)
    grad_key = norm_back(key_norm, key_inv, grad_key * key_gains, HD)
    grad_kv = jnp.concatenate([grad_key, grad_value], axis=1).astype(BF)
    dkv_out[...] = grad_kv
    wkv_s[...] = dot(rows_t, grad_kv, 1, 0).astype(BF)
    kv_part = dot(grad_kv, kv_weights(watt), 1, 1)
    grad_gin = jnp.sum(kv_part * normed_ref[...], axis=0, keepdims=True)
    grad_gin = grad_gin + jnp.sum(part * normed_ref[2 * ROWS :], axis=0, keepdims=True)
    model = jnp.concatenate([grad_gin, sums_ref[1:8], jnp.zeros((120, DP), F32)], axis=0)
    zeros = jnp.zeros((1, HD), F32)
    heads = jnp.concatenate(
        [zeros, zeros, zeros, zeros, grad_gq, grad_gk, zeros, zeros, jnp.zeros((120, HD), F32)],
        axis=0,
    )
    gains = dot(spread, model.astype(BF), 1, 1) + dot(heads_ref[...], heads.astype(BF), 1, 1)
    gains = gains.astype(BF)
    core = core_ref[0]
    own_kv = jnp.broadcast_to(core, (DM, 128)) == 0
    for x in range(XS):
        for out, half in ((keep_out, core), (away_out, 1 - core)):
            cols = pl.ds(pl.multiple_of(x * 256 + half * 128, 128), 128)
            out[:, x, :, 0:128] = wq_s[:, cols].astype(F32).reshape(16, 40, 128).astype(BF)
            out[:, x, :, 128:256] = wo_s[:, cols].astype(F32).reshape(16, 40, 128).astype(BF)
        kv = wkv_s[:, x * 128 : (x + 1) * 128].astype(F32)
        kept = jnp.where(own_kv, kv, gains.astype(F32)).reshape(16, 40, 128).astype(BF)
        sent = jnp.where(own_kv, gains.astype(F32), kv).reshape(16, 40, 128).astype(BF)
        keep_out[:, x, :, 256:384] = kept
        away_out[:, x, :, 256:384] = sent


def call(kernel, outs, args, scratch=(), word=None, weights=None, flops=0):
    whole = pl.BlockSpec(memory_space=pltpu.VMEM)
    first, first_specs = [], []
    if word is not None:
        first, first_specs = [word], [pl.BlockSpec(memory_space=pltpu.SMEM)]
    shapes = [pltpu.VMEM(shape, kind) for shape, kind in scratch]
    if weights is not None:
        gathered, size = weights
        first, first_specs = first + [gathered], first_specs + [pl.BlockSpec(memory_space=pl.ANY)]
        shapes += [pltpu.VMEM((XS, DPS, PAD, size), BF), pltpu.SemaphoreType.DMA((XS,))]
    return pl.pallas_call(
        kernel,
        out_shape=[jax.ShapeDtypeStruct(shape, kind) for shape, kind in outs],
        in_specs=first_specs + [whole] * len(args),
        out_specs=[whole] * len(outs),
        scratch_shapes=shapes,
        compiler_params=pltpu.CompilerParams(vmem_limit_bytes=VMEM),
        cost_estimate=pl.CostEstimate(flops=flops, bytes_accessed=20 * 2**20, transcendentals=0),
    )(*first, *args)


def per_device(
    hidden_in,
    out_grad,
    segment_ids,
    gain_input,
    w_query,
    w_key,
    w_value,
    gain_query,
    gain_key,
    w_out,
    gain_attn,
    gain_ffin,
    w_gate,
    w_up,
    w_down,
    gain_ffout,
):
    at = lax.axis_index("x")
    core = lax.axis_index("core")

    gains_own = jnp.zeros((128, 128), F32)
    for row, gain in enumerate(
        (gain_input, gain_attn, gain_ffin, gain_ffout, gain_query, gain_key)
    ):
        size = gain.shape[0]
        gains_own = gains_own + jnp.pad(
            gain.astype(F32)[None], ((row, 127 - row), (0, 128 - size))
        )
    width = ATT + FFC
    at_word = at.astype(jnp.int32).reshape(1)
    whole = pl.BlockSpec(memory_space=pltpu.VMEM)
    packed = pl.pallas_call(
        pack_kernel,
        out_shape=jax.ShapeDtypeStruct((PAD, width), BF),
        in_specs=[whole] * 8 + [pl.BlockSpec(memory_space=pltpu.SMEM)],
        out_specs=whole,
    )(w_query, w_out, w_gate, w_up, w_down, w_key, w_value, gains_own, at_word)
    gathered = lax.all_gather(packed, EVERY, axis=0, tiled=False).reshape(DPS, XS, PAD, width)

    before_one = lax.ppermute(hidden_in, "x", [(i, i + 1) for i in range(XS - 1)])
    before_two = lax.ppermute(hidden_in, "x", [(i, i + 2) for i in range(XS - 2)])
    rows_low = jnp.concatenate([before_two, before_one, hidden_in], axis=0)
    spread = spread_matrix()
    resid_all = dot(rows_low, spread, 1, 0)
    upstream = dot(out_grad, spread, 1, 0)
    normed_all, inverse_all = norm_of(resid_all, DM)
    resid_in = resid_all[2 * ROWS :]

    offsets = jnp.arange(segment_ids.shape[0], dtype=jnp.int32)
    live = segment_ids >= 0
    tail_start = jnp.sum(live.astype(jnp.int32))
    positions = offsets - jnp.where(live, segment_ids, tail_start)
    positions = jnp.concatenate([jnp.zeros((2 * ROWS,), jnp.int32), positions], axis=0)
    positions = lax.dynamic_slice_in_dim(positions, at * ROWS, KEYS, 0)
    frequency = ROPE_BASE ** (-2.0 * jnp.arange(HALF, dtype=F32) / HD)
    angles = positions.astype(F32)[:, None] * frequency[None, :]
    cosine, sine = jnp.cos(angles), jnp.sin(angles)
    ids = jnp.concatenate([jnp.full((2 * ROWS,), -2, jnp.int32), segment_ids], axis=0)
    key_ids = lax.dynamic_slice_in_dim(ids, at * ROWS, KEYS, 0)
    query_ids = key_ids[2 * ROWS :]
    row_at = lax.broadcasted_iota(jnp.int32, (ROWS, KEYS), 0)
    col_at = lax.broadcasted_iota(jnp.int32, (ROWS, KEYS), 1)
    gap = row_at + 2 * ROWS - col_at
    visible = (
        (query_ids[:, None] == key_ids[None, :])
        & (gap >= 0)
        & (gap < WINDOW)
        & ((query_ids[:, None] >= 0) | (gap == 0))
    )
    bias = jnp.where(visible, 0.0, NEGATIVE).astype(F32)

    gains, rows_all, query_raw, kv_raw, query, key, value, probs, mixed, attn_sum = call(
        attend_kernel,
        [
            ((16, DP), F32),
            ((KEYS, DP), BF),
            ((ROWS, HQ * HD), F32),
            ((KEYS, 2 * HD), F32),
            ((ROWS, HQ * HD), BF),
            ((KEYS, HD), BF),
            ((KEYS, HD), BF),
            ((HQ, ROWS, KEYS), F32),
            ((ROWS, HQ * HD), BF),
            ((ROWS, DP), F32),
        ],
        [normed_all, cosine, sine, bias, head_matrix(PAD)],
        weights=(gathered, ATT),
        flops=2 * 10**9,
    )
    core_word = core.astype(jnp.int32).reshape(1)
    layer_out, grad_resid, grad_attn, away_ff, sums, *feed = call(
        feed_kernel,
        [
            ((ROWS, DM), BF),
            ((ROWS, DP), F32),
            ((ROWS, DP), BF),
            ((16, XS, 40, 768), BF),
            ((8, DP), F32),
            ((ROWS, 2048), BF),
            ((ROWS, 2048), BF),
            ((ROWS, 2048), BF),
            ((DM, ROWS), BF),
            ((DM, ROWS), BF),
        ],
        [attn_sum, resid_in, upstream, gains, spread],
        [((ROWS, 2048), F32), ((ROWS, 2048), F32)],
        word=core_word,
        weights=(gathered, FFC),
        flops=8 * 10**9,
    )
    swap = [(0, 1), (1, 0)]
    arrived_ff = lax.ppermute(away_ff, "core", swap)
    (keep_ff,) = call(
        feed_keep_kernel, [((16, XS, 40, 768), BF)], feed, word=core_word, flops=2 * 10**9
    )
    both_ff = add_low(keep_ff, arrived_ff)
    both_ff, grad_attn = lax.optimization_barrier((both_ff, grad_attn))
    parts_ff = lax.all_to_all(both_ff, CHIP, 0, 0, tiled=True)
    keep_att, away_att, grad_kv, query_part = call(
        attend_back_kernel,
        [
            ((16, XS, 40, 384), BF),
            ((16, XS, 40, 384), BF),
            ((KEYS, 2 * HD), BF),
            ((ROWS, DP), F32),
        ],
        [
            grad_attn, rows_all, normed_all, query_raw, kv_raw, query, key, value, probs, mixed,
            cosine, sine, gains, sums, spread, head_matrix(OWN),
        ],
        [((DM, 1024), BF), ((DM, 1024), BF), ((DM, 512), BF)],
        word=core_word,
        weights=(gathered, ATT),
        flops=4 * 10**9,
    )
    arrived_att = lax.ppermute(away_att, "core", swap)
    from_one = lax.ppermute(
        grad_kv[ROWS : 2 * ROWS], "x", [(i + 1, i) for i in range(XS - 1)]
    )
    from_two = lax.ppermute(grad_kv[:ROWS], "x", [(i + 2, i) for i in range(XS - 2)])
    both_att = add_low(keep_att, arrived_att)
    both_att, parts_ff, from_one, from_two = lax.optimization_barrier(
        (both_att, parts_ff, from_one, from_two)
    )
    parts_att = lax.all_to_all(both_att, CHIP, 0, 0, tiled=True)
    total_ff = jnp.sum(parts_ff.astype(F32), axis=0)
    total_att = jnp.sum(parts_att.astype(F32), axis=0)

    grad_kv_own = (
        grad_kv[2 * ROWS :].astype(F32) + from_one.astype(F32) + from_two.astype(F32)
    ).astype(BF)
    kv_cols = gathered[:, :, :, 512:640].transpose(0, 2, 1, 3).reshape(DP, 2 * HD)
    grad_in = query_part + dot(grad_kv_own, kv_cols, 1, 1)
    normed_in, inverse_in = normed_all[2 * ROWS :], inverse_all[2 * ROWS :]
    input_grad = grad_resid + norm_back(normed_in, inverse_in, grad_in * gains[0:1], DM)
    grad_top = input_grad.astype(BF)
    grad_rest = (input_grad - grad_top.astype(F32)).astype(BF)
    input_grad = dot(grad_top, spread, 1, 1) + dot(grad_rest, spread, 1, 1)

    total = jnp.concatenate([total_ff, total_att], axis=1)
    kv = total[:, 1024:]
    kv = jnp.concatenate(
        [kv] + [lax.ppermute(kv, "x", [(i, (i + s) % XS) for i in range(XS)]) for s in (3, 2, 1)],
        axis=1,
    )
    kv = jnp.concatenate([kv, kv], axis=1)
    kv = lax.dynamic_slice_in_dim(kv, ((XS - at) % XS) * 128, 512, 1)
    total = jnp.concatenate([total, kv], axis=1)
    mine = lax.dynamic_slice_in_dim(total, core * OWN, OWN, 0)
    other = lax.ppermute(lax.dynamic_slice_in_dim(total, (1 - core) * OWN, OWN, 0), "core", swap)
    left = jnp.where(core == 0, mine, other)
    right = jnp.where(core == 0, other, mine)

    def join(first, size):
        return jnp.concatenate([left[:, first : first + size], right[:, first : first + size]], 1)

    gains_total = right[:, 1024:1152]
    return (
        layer_out,
        input_grad,
        gains_total[:, 0],
        join(768, 128)[:, None, :],
        left[:, 1152:1408],
        left[:, 1408:1664],
        gains_total[:8, 4],
        gains_total[:8, 5],
        join(896, 128)[:, None, :],
        gains_total[:, 1],
        gains_total[:, 2],
        join(0, 256),
        join(256, 256),
        join(512, 256),
        gains_total[:, 3],
    )


def add_low(keep, arrived):
    both = (keep.astype(F32) + arrived.astype(F32)).astype(BF)
    return both.reshape(64, 40, both.shape[-1])


def solution(mesh):
    fine = Mesh(mesh.devices.reshape(ZS, YS, CS, XS), EVERY)
    dp = ("z", "y", "core")
    in_specs = (
        P(EVERY, None),
        P(EVERY, None),
        P(dp),
        P(dp),
        P(dp, "x", None),
        P(dp, None),
        P(dp, None),
        P(dp),
        P(dp),
        P(dp, "x", None),
        P(dp),
        P(dp),
        P(dp, "x"),
        P(dp, "x"),
        P(dp, "x"),
        P(dp),
    )
    out_specs = (
        P(EVERY, None),
        P(EVERY, None),
        P(dp),
        P(dp, "x", None),
        P(dp, None),
        P(dp, None),
        P(dp),
        P(dp),
        P(dp, "x", None),
        P(dp),
        P(dp),
        P(dp, "x"),
        P(dp, "x"),
        P(dp, "x"),
        P(dp),
    )
    return jax.shard_map(
        per_device, mesh=fine, in_specs=in_specs, out_specs=out_specs, check_vma=False
    )
```

```python
import jax
import jax.numpy as jnp
from jax import lax
from jax.experimental import pallas as pl
from jax.experimental.pallas import tpu as pltpu
from jax.sharding import Mesh, PartitionSpec as P

WINDOW = 512
EPS = 1e-06
ROPE_BASE = 10000.0
NEGATIVE = -1e30
ZS, YS, CS, XS = 4, 4, 2, 4
CHIP = ("z", "y", "x")
EVERY = ("z", "y", "core", "x")
DPS = 32
OWN = 20
PAD = 24
DM = 640
DP = DPS * PAD
ROWS = 256
KEYS = 3 * ROWS
HQ = 4
HD = 256
HALF = HD // 2
ATT = 768
FFC = 1536
SCALE = HD**-0.5
GELU_C = 0.7978845608028654
GELU_A = 0.044715
BF = jnp.bfloat16
F32 = jnp.float32


def norm_of(values_in, width):
    inverse = lax.rsqrt(
        jnp.sum(values_in * values_in, axis=-1, keepdims=True) * (1.0 / width) + EPS
    )
    return values_in * inverse, inverse


def norm_back(normed, inverse, upstream, width):
    mean = jnp.sum(upstream * normed, axis=-1, keepdims=True) * (1.0 / width)
    return inverse * (upstream - normed * mean)


def rotate(values_in, cosine, sine):
    first, second = values_in[:, :HALF], values_in[:, HALF:]
    return jnp.concatenate(
        [first * cosine - second * sine, second * cosine + first * sine], axis=1
    )


def dot(lhs, rhs, lhs_dim, rhs_dim):
    return lax.dot_general(
        lhs, rhs, (((lhs_dim,), (rhs_dim,)), ((), ())), preferred_element_type=F32
    )


def spread_matrix():
    row = lax.broadcasted_iota(jnp.int32, (DM, DP), 0)
    col = lax.broadcasted_iota(jnp.int32, (DM, DP), 1)
    return ((col % PAD < OWN) & (row == (col // PAD) * OWN + col % PAD)).astype(BF)


def head_matrix(step):
    row = lax.broadcasted_iota(jnp.int32, (DPS * step, HD), 0)
    col = lax.broadcasted_iota(jnp.int32, (DPS * step, HD), 1)
    return ((row // step == col // 8) & (row % step == col % 8)).astype(BF)


def fetch(gathered, held, sems, first, size):
    copies = [
        pltpu.make_async_copy(gathered.at[:, x, :, first : first + size], held.at[x], sems.at[x])
        for x in range(XS)
    ]
    for copy in copies:
        copy.start()
    return copies


def cut(held, x, first, size):
    return held[x, :, :, first : first + size].reshape(DP, size)


def kv_weights(watt):
    return jnp.concatenate([cut(watt, x, 512, 128) for x in range(XS)], axis=1)


def pack_kernel(wqo_ref, wg_ref, wu_ref, wd_ref, wk_ref, wv_ref, gains_ref, at_ref, out):
    out[...] = jnp.zeros(out.shape, BF)
    out[0:OWN, 0:512] = wqo_ref[...]
    at = at_ref[0]
    kv = jnp.where(
        jnp.broadcast_to(at, (OWN, 256)) < 2, wk_ref[...].astype(F32), wv_ref[...].astype(F32)
    )
    kv = jnp.where(jnp.broadcast_to(at % 2, (OWN, 128)) == 0, kv[:, :128], kv[:, 128:])
    out[0:OWN, 512:640] = kv.astype(BF)
    out[:, 640:768] = gains_ref[...].T[:PAD].astype(BF)
    out[0:OWN, 768:1280] = wg_ref[...]
    out[0:OWN, 1280:1792] = wu_ref[...]
    out[0:OWN, 1792:2304] = wd_ref[...]


def forward_kernel(
    core_ref, gathered, normed_ref, cosine_ref, sine_ref, bias_ref, heads_ref, resid_ref, up_ref,
    spread_ref,
    gains_out, rows_out, qraw_out, kvraw_out, q_out, k_out, v_out, probs_out, mixed_out,
    layer_out, dres_out, dattn_out, away_out, sums_out, z_s, dg_s, du_s, rows_t_out, ff_t_out,
    attn_t_out, gate_s, upp_s, watt, sems, wff, ff_sems,
):
    attend_copies = fetch(gathered, watt, sems, 0, ATT)
    copies = fetch(gathered, wff, ff_sems, ATT, FFC)
    for copy in attend_copies:
        copy.wait()
    gains = cut(watt, 0, 640, 128).astype(F32).T
    gains_out[0:8] = gains[0:8]
    head_gains = dot(gains.astype(BF), heads_ref[...], 1, 0)
    gains_out[8:16] = jnp.concatenate([head_gains[0:8]] * 3, axis=1)
    query_gains, key_gains = head_gains[4:5], head_gains[5:6]
    rows = (normed_ref[...] * gains[0:1]).astype(BF)
    rows_out[...] = rows
    kv_raw = dot(rows, kv_weights(watt), 1, 0)
    kvraw_out[...] = kv_raw
    key_norm, _ = norm_of(kv_raw[:, :HD], HD)
    key = rotate(key_norm * key_gains, cosine_ref[...], sine_ref[...]).astype(BF)
    value = kv_raw[:, HD:].astype(BF)
    k_out[...] = key
    v_out[...] = value
    rows_own = rows[2 * ROWS :]
    cosine, sine = cosine_ref[2 * ROWS :], sine_ref[2 * ROWS :]
    attn = jnp.zeros((ROWS, DP), F32)
    for head in range(HQ):
        at = slice(head * HD, (head + 1) * HD)
        query_raw = dot(rows_own, cut(watt, head, 0, 256), 1, 0)
        qraw_out[:, at] = query_raw
        query_norm, _ = norm_of(query_raw, HD)
        query = rotate(query_norm * query_gains, cosine, sine).astype(BF)
        q_out[:, at] = query
        scores = dot(query, key, 1, 1) * SCALE + bias_ref[...]
        exponent = jnp.exp(scores - jnp.max(scores, axis=-1, keepdims=True))
        probs = exponent * (1.0 / jnp.sum(exponent, axis=-1, keepdims=True))
        probs = probs.astype(BF)
        probs_out[head] = probs
        mixed = dot(probs, value, 1, 0).astype(BF)
        mixed_out[:, at] = mixed
        attn = attn + dot(mixed, cut(watt, head, 256, 256), 1, 1)
    attn_gains, ffin_gains, ffout_gains = gains[1:2], gains[2:3], gains[3:4]
    spread = spread_ref[...]
    upstream = up_ref[...]
    attn_normed, attn_inv = norm_of(attn, DM)
    mid = resid_ref[...] + attn_normed * attn_gains
    mid_normed, mid_inv = norm_of(mid, DM)
    rows = (mid_normed * ffin_gains).astype(BF)
    ff_sum = jnp.zeros((ROWS, DP), F32)
    for x in range(XS):
        at = slice(x * 512, (x + 1) * 512)
        copies[x].wait()
        gate = dot(rows, cut(wff, x, 0, 512), 1, 0)
        up = dot(rows, cut(wff, x, 512, 512), 1, 0)
        gate_s[:, at] = gate
        upp_s[:, at] = up
        act = 0.5 * gate * (1.0 + jnp.tanh(GELU_C * (gate + GELU_A * gate * gate * gate)))
        hidden = (act * up).astype(BF)
        z_s[:, at] = hidden
        ff_sum = ff_sum + dot(hidden, cut(wff, x, 1024, 512), 1, 1)
    ff_normed, ff_inv = norm_of(ff_sum, DM)
    layer = (mid + ff_normed * ffout_gains).astype(BF)
    layer_out[...] = dot(layer, spread, 1, 1).astype(BF)
    grad_gout = jnp.sum(upstream * ff_normed, axis=0, keepdims=True)
    grad_ff = norm_back(ff_normed, ff_inv, upstream * ffout_gains, DM).astype(BF)
    grad_mid = jnp.zeros((ROWS, DP), F32)
    for x in range(XS):
        at = slice(x * 512, (x + 1) * 512)
        grad_hidden = dot(grad_ff, cut(wff, x, 1024, 512), 1, 0)
        gate, up = gate_s[:, at], upp_s[:, at]
        curve = jnp.tanh(GELU_C * (gate + GELU_A * gate * gate * gate))
        slope = 0.5 * (1.0 + curve) + 0.5 * gate * (1.0 - curve * curve) * (
            GELU_C * (1.0 + 3.0 * GELU_A * gate * gate)
        )
        grad_gate = (grad_hidden * up * slope).astype(BF)
        grad_up = (grad_hidden * (0.5 * gate * (1.0 + curve))).astype(BF)
        dg_s[:, at] = grad_gate
        du_s[:, at] = grad_up
        grad_mid = grad_mid + dot(grad_gate, cut(wff, x, 0, 512), 1, 1)
        grad_mid = grad_mid + dot(grad_up, cut(wff, x, 512, 512), 1, 1)
    grad_gfin = jnp.sum(grad_mid * mid_normed, axis=0, keepdims=True)
    grad_resid = upstream + norm_back(mid_normed, mid_inv, grad_mid * ffin_gains, DM)
    dres_out[...] = grad_resid
    grad_gattn = jnp.sum(grad_resid * attn_normed, axis=0, keepdims=True)
    dattn_out[...] = norm_back(attn_normed, attn_inv, grad_resid * attn_gains, DM).astype(BF)
    zero = jnp.zeros((1, DP), F32)
    sums_out[...] = jnp.concatenate(
        [zero, grad_gattn, grad_gfin, grad_gout, zero, zero, zero, zero], axis=0
    )
    rows_t = dot(spread, rows, 1, 1).astype(BF)
    ff_t = dot(spread, grad_ff, 1, 1).astype(BF)
    attn_t = dot(spread, dattn_out[...], 1, 1).astype(BF)
    rows_t_out[...] = rows_t
    ff_t_out[...] = ff_t
    attn_t_out[...] = attn_t
    feed_half(1 - core_ref[0], away_out, rows_t, ff_t, attn_t, z_s, dg_s, du_s, mixed_out)


def feed_half(half, out, rows_t, ff_t, attn_t, z_ref, dg_ref, du_ref, mixed_ref):
    for x in range(XS):
        cols = pl.ds(pl.multiple_of(x * 512 + half * 256, 256), 256)
        for part, (lhs, rhs) in enumerate(((rows_t, dg_ref), (rows_t, du_ref), (ff_t, z_ref))):
            grad = dot(lhs, rhs[:, cols], 1, 0).astype(BF)
            out[x, :, part * 256 : (part + 1) * 256] = grad
        cols = pl.ds(pl.multiple_of(x * 256 + half * 128, 128), 128)
        out[x, :, 768:896] = dot(attn_t, mixed_ref[:, cols], 1, 0).astype(BF)


def feed_keep_kernel(
    core_ref, z_ref, dg_ref, du_ref, rows_t_ref, ff_t_ref, attn_t_ref, mixed_ref, keep_out
):
    feed_half(
        core_ref[0], keep_out, rows_t_ref[...], ff_t_ref[...], attn_t_ref[...],
        z_ref, dg_ref, du_ref, mixed_ref,
    )


def attend_back_kernel(
    core_ref, gathered, dattn_ref, rows_ref, normed_ref, qraw_ref, kvraw_ref, q_ref, k_ref, v_ref,
    probs_ref, cosine_ref, sine_ref, gains_ref, sums_ref, spread_ref, heads_ref,
    keep_out, away_out, dkv_out, part_out, wq_s, wkv_s, watt, sems,
):
    copies = fetch(gathered, watt, sems, 0, ATT)
    spread = spread_ref[...]
    query_gains, key_gains = gains_ref[12:13, :HD], gains_ref[13:14, :HD]
    grad_attn = dattn_ref[...]
    rows_t = dot(spread, rows_ref[...], 1, 1).astype(BF)
    rows_own_t = rows_t[:, 2 * ROWS :]
    key, value = k_ref[...], v_ref[...]
    cosine, sine = cosine_ref[2 * ROWS :], sine_ref[2 * ROWS :]
    for copy in copies:
        copy.wait()
    grad_key = jnp.zeros((KEYS, HD), F32)
    grad_value = jnp.zeros((KEYS, HD), F32)
    part = jnp.zeros((ROWS, DP), F32)
    grad_gq = jnp.zeros((1, HD), F32)
    for head in range(HQ):
        at = slice(head * HD, (head + 1) * HD)
        grad_mixed = dot(grad_attn, cut(watt, head, 256, 256), 1, 0).astype(BF)
        probs_low = probs_ref[head]
        probs = probs_low.astype(F32)
        grad_value = grad_value + dot(probs_low, grad_mixed, 0, 0)
        grad_probs = dot(grad_mixed, value, 1, 1)
        grad_scores = (
            probs * (grad_probs - jnp.sum(probs * grad_probs, axis=-1, keepdims=True))
        ).astype(BF)
        grad_query = dot(grad_scores, key, 1, 0) * SCALE
        grad_key = grad_key + dot(grad_scores, q_ref[:, at], 0, 0)
        query_norm, query_inv = norm_of(qraw_ref[:, at], HD)
        grad_query = rotate(grad_query, cosine, -sine)
        grad_gq = grad_gq + jnp.sum(grad_query * query_norm, axis=0, keepdims=True)
        grad_raw = norm_back(query_norm, query_inv, grad_query * query_gains, HD).astype(BF)
        part = part + dot(grad_raw, cut(watt, head, 0, 256), 1, 1)
        wq_s[:, at] = dot(rows_own_t, grad_raw, 1, 0).astype(BF)
    part_out[...] = part
    key_norm, key_inv = norm_of(kvraw_ref[:, :HD], HD)
    grad_key = rotate(grad_key * SCALE, cosine_ref[...], -sine_ref[...])
    grad_gk = jnp.sum(grad_key * key_norm, axis=0, keepdims=True)
    grad_key = norm_back(key_norm, key_inv, grad_key * key_gains, HD)
    grad_kv = jnp.concatenate([grad_key, grad_value], axis=1).astype(BF)
    dkv_out[...] = grad_kv
    wkv_s[...] = dot(rows_t, grad_kv, 1, 0).astype(BF)
    kv_part = dot(grad_kv, kv_weights(watt), 1, 1)
    grad_gin = jnp.sum(kv_part * normed_ref[...], axis=0, keepdims=True)
    grad_gin = grad_gin + jnp.sum(part * normed_ref[2 * ROWS :], axis=0, keepdims=True)
    model = jnp.concatenate([grad_gin, sums_ref[1:8], jnp.zeros((120, DP), F32)], axis=0)
    zeros = jnp.zeros((1, HD), F32)
    heads = jnp.concatenate(
        [zeros, zeros, zeros, zeros, grad_gq, grad_gk, zeros, zeros, jnp.zeros((120, HD), F32)],
        axis=0,
    )
    gains = dot(spread, model.astype(BF), 1, 1) + dot(heads_ref[...], heads.astype(BF), 1, 1)
    gains = gains.astype(BF)
    core = core_ref[0]
    own_kv = jnp.broadcast_to(core, (DM, 128)) == 0
    for x in range(XS):
        for out, half in ((keep_out, core), (away_out, 1 - core)):
            cols = pl.ds(pl.multiple_of(x * 256 + half * 128, 128), 128)
            out[:, x, :, 0:128] = wq_s[:, cols].astype(F32).reshape(16, 40, 128).astype(BF)
        kv = wkv_s[:, x * 128 : (x + 1) * 128].astype(F32)
        kept = jnp.where(own_kv, kv, gains.astype(F32)).reshape(16, 40, 128).astype(BF)
        sent = jnp.where(own_kv, gains.astype(F32), kv).reshape(16, 40, 128).astype(BF)
        keep_out[:, x, :, 128:256] = kept
        away_out[:, x, :, 128:256] = sent


def call(kernel, outs, args, scratch=(), word=None, weights=None, flops=0, vmem=0):
    whole = pl.BlockSpec(memory_space=pltpu.VMEM)
    first, first_specs = [], []
    if word is not None:
        first, first_specs = [word], [pl.BlockSpec(memory_space=pltpu.SMEM)]
    shapes = [pltpu.VMEM(shape, kind) for shape, kind in scratch]
    if weights is not None:
        gathered, *sizes = weights
        first, first_specs = first + [gathered], first_specs + [pl.BlockSpec(memory_space=pl.ANY)]
        for size in sizes:
            shapes += [pltpu.VMEM((XS, DPS, PAD, size), BF), pltpu.SemaphoreType.DMA((XS,))]
    return pl.pallas_call(
        kernel,
        out_shape=[jax.ShapeDtypeStruct(shape, kind) for shape, kind in outs],
        in_specs=first_specs + [whole] * len(args),
        out_specs=[whole] * len(outs),
        scratch_shapes=shapes,
        compiler_params=pltpu.CompilerParams(vmem_limit_bytes=vmem * 2**20),
        cost_estimate=pl.CostEstimate(flops=flops, bytes_accessed=20 * 2**20, transcendentals=0),
    )(*first, *args)


def per_device(
    hidden_in,
    out_grad,
    segment_ids,
    gain_input,
    w_query,
    w_key,
    w_value,
    gain_query,
    gain_key,
    w_out,
    gain_attn,
    gain_ffin,
    w_gate,
    w_up,
    w_down,
    gain_ffout,
):
    at = lax.axis_index("x")
    core = lax.axis_index("core")

    gains_own = jnp.zeros((128, 128), F32)
    for row, gain in enumerate(
        (gain_input, gain_attn, gain_ffin, gain_ffout, gain_query, gain_key)
    ):
        size = gain.shape[0]
        gains_own = gains_own + jnp.pad(
            gain.astype(F32)[None], ((row, 127 - row), (0, 128 - size))
        )
    width = ATT + FFC
    at_word = at.astype(jnp.int32).reshape(1)
    whole = pl.BlockSpec(memory_space=pltpu.VMEM)
    packed = pl.pallas_call(
        pack_kernel,
        out_shape=jax.ShapeDtypeStruct((PAD, width), BF),
        in_specs=[whole] * 7 + [pl.BlockSpec(memory_space=pltpu.SMEM)],
        out_specs=whole,
    )(jnp.concatenate([w_query[:, 0], w_out[:, 0]], axis=1), w_gate, w_up, w_down, w_key, w_value, gains_own, at_word)
    gathered = lax.all_gather(packed, EVERY, axis=0, tiled=False).reshape(DPS, XS, PAD, width)

    before_one = lax.ppermute(hidden_in, "x", [(i, i + 1) for i in range(XS - 1)])
    before_two = lax.ppermute(hidden_in, "x", [(i, i + 2) for i in range(XS - 2)])
    rows_low = jnp.concatenate([before_two, before_one, hidden_in], axis=0)
    spread = spread_matrix()
    resid_all = dot(rows_low, spread, 1, 0)
    upstream = dot(out_grad, spread, 1, 0)
    normed_all, inverse_all = norm_of(resid_all, DM)
    resid_in = resid_all[2 * ROWS :]

    offsets = jnp.arange(segment_ids.shape[0], dtype=jnp.int32)
    live = segment_ids >= 0
    tail_start = jnp.sum(live.astype(jnp.int32))
    positions = offsets - jnp.where(live, segment_ids, tail_start)
    positions = jnp.concatenate([jnp.zeros((2 * ROWS,), jnp.int32), positions], axis=0)
    positions = lax.dynamic_slice_in_dim(positions, at * ROWS, KEYS, 0)
    frequency = ROPE_BASE ** (-2.0 * jnp.arange(HALF, dtype=F32) / HD)
    angles = positions.astype(F32)[:, None] * frequency[None, :]
    cosine, sine = jnp.cos(angles), jnp.sin(angles)
    ids = jnp.concatenate([jnp.full((2 * ROWS,), -2, jnp.int32), segment_ids], axis=0)
    key_ids = lax.dynamic_slice_in_dim(ids, at * ROWS, KEYS, 0)
    query_ids = key_ids[2 * ROWS :]
    row_at = lax.broadcasted_iota(jnp.int32, (ROWS, KEYS), 0)
    col_at = lax.broadcasted_iota(jnp.int32, (ROWS, KEYS), 1)
    gap = row_at + 2 * ROWS - col_at
    visible = (
        (query_ids[:, None] == key_ids[None, :])
        & (gap >= 0)
        & (gap < WINDOW)
        & ((query_ids[:, None] >= 0) | (gap == 0))
    )
    bias = jnp.where(visible, 0.0, NEGATIVE).astype(F32)

    core_word = core.astype(jnp.int32).reshape(1)
    (
        gains, rows_all, query_raw, kv_raw, query, key, value, probs, mixed,
        layer_out, grad_resid, grad_attn, away_ff, sums, *feed,
    ) = call(
        forward_kernel,
        [
            ((16, DP), F32),
            ((KEYS, DP), BF),
            ((ROWS, HQ * HD), F32),
            ((KEYS, 2 * HD), F32),
            ((ROWS, HQ * HD), BF),
            ((KEYS, HD), BF),
            ((KEYS, HD), BF),
            ((HQ, ROWS, KEYS), BF),
            ((ROWS, HQ * HD), BF),
            ((ROWS, DM), BF),
            ((ROWS, DP), F32),
            ((ROWS, DP), BF),
            ((XS, DM, 896), BF),
            ((8, DP), F32),
            ((ROWS, 2048), BF),
            ((ROWS, 2048), BF),
            ((ROWS, 2048), BF),
            ((DM, ROWS), BF),
            ((DM, ROWS), BF),
            ((DM, ROWS), BF),
        ],
        [normed_all, cosine, sine, bias, head_matrix(PAD), resid_in, upstream, spread],
        [((ROWS, 2048), F32), ((ROWS, 2048), F32)],
        word=core_word,
        weights=(gathered, ATT, FFC),
        flops=10**10,
        vmem=46,
    )
    swap = [(0, 1), (1, 0)]
    arrived_ff = lax.ppermute(away_ff, "core", swap)
    (keep_ff,) = call(
        feed_keep_kernel, [((XS, DM, 896), BF)], feed + [mixed], word=core_word, flops=2 * 10**9, vmem=20
    )
    both_ff = (keep_ff.astype(F32) + arrived_ff.astype(F32)).astype(BF)
    both_ff, grad_attn = lax.optimization_barrier((both_ff, grad_attn))
    column_ff = lax.psum_scatter(
        both_ff.reshape(XS * DM, 896), "x", scatter_dimension=0, tiled=True
    )
    keep_att, away_att, grad_kv, query_part = call(
        attend_back_kernel,
        [
            ((16, XS, 40, 256), BF),
            ((16, XS, 40, 256), BF),
            ((KEYS, 2 * HD), BF),
            ((ROWS, DP), F32),
        ],
        [
            grad_attn, rows_all, normed_all, query_raw, kv_raw, query, key, value, probs,
            cosine, sine, gains, sums, spread, head_matrix(OWN),
        ],
        [((DM, 1024), BF), ((DM, 512), BF)],
        word=core_word,
        weights=(gathered, ATT),
        flops=4 * 10**9,
        vmem=60,
    )
    arrived_att = lax.ppermute(away_att, "core", swap)
    from_one = lax.ppermute(
        grad_kv[ROWS : 2 * ROWS], "x", [(i + 1, i) for i in range(XS - 1)]
    )
    from_two = lax.ppermute(grad_kv[:ROWS], "x", [(i + 2, i) for i in range(XS - 2)])
    both_att = (keep_att.astype(F32) + arrived_att.astype(F32)).astype(BF)
    parts_att = lax.all_to_all(both_att.reshape(16, 160, 256), ("z", "y"), 0, 0, tiled=True)
    parts_att, column_ff = lax.optimization_barrier((parts_att, column_ff))
    row_att = jnp.sum(parts_att.astype(F32), axis=0).astype(BF)
    total_att = lax.psum_scatter(row_att, "x", scatter_dimension=0, tiled=True).astype(F32)
    parts_ff = lax.all_to_all(column_ff.reshape(16, 40, 896), ("z", "y"), 0, 0, tiled=True)
    total_ff = jnp.sum(parts_ff.astype(F32), axis=0)
    total = jnp.concatenate([total_ff, total_att], axis=1)

    grad_kv_own = (
        grad_kv[2 * ROWS :].astype(F32) + from_one.astype(F32) + from_two.astype(F32)
    ).astype(BF)
    kv_cols = gathered[:, :, :, 512:640].transpose(0, 2, 1, 3).reshape(DP, 2 * HD)
    grad_in = query_part + dot(grad_kv_own, kv_cols, 1, 1)
    normed_in, inverse_in = normed_all[2 * ROWS :], inverse_all[2 * ROWS :]
    input_grad = grad_resid + norm_back(normed_in, inverse_in, grad_in * gains[0:1], DM)
    grad_top = input_grad.astype(BF)
    grad_rest = (input_grad - grad_top.astype(F32)).astype(BF)
    input_grad = dot(grad_top, spread, 1, 1) + dot(grad_rest, spread, 1, 1)

    kv = total[:, 1024:]
    kv = jnp.concatenate(
        [kv] + [lax.ppermute(kv, "x", [(i, (i + s) % XS) for i in range(XS)]) for s in (3, 2, 1)],
        axis=1,
    )
    kv = jnp.concatenate([kv, kv], axis=1)
    kv = lax.dynamic_slice_in_dim(kv, ((XS - at) % XS) * 128, 512, 1)
    total = jnp.concatenate([total, kv], axis=1)
    mine = lax.dynamic_slice_in_dim(total, core * OWN, OWN, 0)
    other = lax.ppermute(lax.dynamic_slice_in_dim(total, (1 - core) * OWN, OWN, 0), "core", swap)
    left = jnp.where(core == 0, mine, other)
    right = jnp.where(core == 0, other, mine)

    def join(first, size):
        return jnp.concatenate([left[:, first : first + size], right[:, first : first + size]], 1)

    gains_total = right[:, 1024:1152]
    return (
        layer_out,
        input_grad,
        gains_total[:, 0],
        join(896, 128)[:, None, :],
        left[:, 1152:1408],
        left[:, 1408:1664],
        gains_total[:8, 4],
        gains_total[:8, 5],
        join(768, 128)[:, None, :],
        gains_total[:, 1],
        gains_total[:, 2],
        join(0, 256),
        join(256, 256),
        join(512, 256),
        gains_total[:, 3],
    )


def solution(mesh):
    fine = Mesh(mesh.devices.reshape(ZS, YS, CS, XS), EVERY)
    dp = ("z", "y", "core")
    in_specs = (
        P(EVERY, None),
        P(EVERY, None),
        P(dp),
        P(dp),
        P(dp, "x", None),
        P(dp, None),
        P(dp, None),
        P(dp),
        P(dp),
        P(dp, "x", None),
        P(dp),
        P(dp),
        P(dp, "x"),
        P(dp, "x"),
        P(dp, "x"),
        P(dp),
    )
    out_specs = (
        P(EVERY, None),
        P(EVERY, None),
        P(dp),
        P(dp, "x", None),
        P(dp, None),
        P(dp, None),
        P(dp),
        P(dp),
        P(dp, "x", None),
        P(dp),
        P(dp),
        P(dp, "x"),
        P(dp, "x"),
        P(dp, "x"),
        P(dp),
    )
    return jax.shard_map(
        per_device, mesh=fine, in_specs=in_specs, out_specs=out_specs, check_vma=False
    )
```

```python
import jax
import jax.numpy as jnp
from jax import lax
from jax.experimental import pallas as pl
from jax.experimental.pallas import tpu as pltpu
from jax.sharding import Mesh, PartitionSpec as P

WINDOW = 512
EPS = 1e-06
ROPE_BASE = 10000.0
NEGATIVE = -1e30
ZS, YS, CS, XS = 4, 4, 2, 4
CHIP = ("z", "y", "x")
EVERY = ("z", "y", "core", "x")
DPS = 32
OWN = 20
PAD = 24
DM = 640
DP = DPS * PAD
ROWS = 256
KEYS = 3 * ROWS
HQ = 4
HD = 256
HALF = HD // 2
ATT = 768
FFC = 1536
SCALE = HD**-0.5
GELU_C = 0.7978845608028654
GELU_A = 0.044715
BF = jnp.bfloat16
F32 = jnp.float32


def norm_of(values_in, width):
    inverse = lax.rsqrt(
        jnp.sum(values_in * values_in, axis=-1, keepdims=True) * (1.0 / width) + EPS
    )
    return values_in * inverse, inverse


def norm_back(normed, inverse, upstream, width):
    mean = jnp.sum(upstream * normed, axis=-1, keepdims=True) * (1.0 / width)
    return inverse * (upstream - normed * mean)


def rotate(values_in, cosine, sine):
    first, second = values_in[:, :HALF], values_in[:, HALF:]
    return jnp.concatenate(
        [first * cosine - second * sine, second * cosine + first * sine], axis=1
    )


def dot(lhs, rhs, lhs_dim, rhs_dim):
    return lax.dot_general(
        lhs, rhs, (((lhs_dim,), (rhs_dim,)), ((), ())), preferred_element_type=F32
    )


def spread_matrix():
    row = lax.broadcasted_iota(jnp.int32, (DM, DP), 0)
    col = lax.broadcasted_iota(jnp.int32, (DM, DP), 1)
    return ((col % PAD < OWN) & (row == (col // PAD) * OWN + col % PAD)).astype(BF)


def head_matrix(step):
    row = lax.broadcasted_iota(jnp.int32, (DPS * step, HD), 0)
    col = lax.broadcasted_iota(jnp.int32, (DPS * step, HD), 1)
    return ((row // step == col // 8) & (row % step == col % 8)).astype(BF)


def fetch(gathered, held, sems, first, size):
    copies = [
        pltpu.make_async_copy(gathered.at[:, x, :, first : first + size], held.at[x], sems.at[x])
        for x in range(XS)
    ]
    for copy in copies:
        copy.start()
    return copies


def cut(held, x, first, size):
    return held[x, :, :, first : first + size].reshape(DP, size)


def kv_weights(watt):
    return jnp.concatenate([cut(watt, x, 512, 128) for x in range(XS)], axis=1)


def pack_kernel(wqo_ref, wg_ref, wu_ref, wd_ref, wk_ref, wv_ref, gains_ref, at_ref, out):
    out[...] = jnp.zeros(out.shape, BF)
    out[0:OWN, 0:512] = wqo_ref[...]
    at = at_ref[0]
    kv = jnp.where(
        jnp.broadcast_to(at, (OWN, 256)) < 2, wk_ref[...].astype(F32), wv_ref[...].astype(F32)
    )
    kv = jnp.where(jnp.broadcast_to(at % 2, (OWN, 128)) == 0, kv[:, :128], kv[:, 128:])
    out[0:OWN, 512:640] = kv.astype(BF)
    out[:, 640:768] = gains_ref[...].T[:PAD].astype(BF)
    out[0:OWN, 768:1280] = wg_ref[...]
    out[0:OWN, 1280:1792] = wu_ref[...]
    out[0:OWN, 1792:2304] = wd_ref[...]


def forward_kernel(
    core_ref, gathered, normed_ref, cosine_ref, sine_ref, bias_ref, heads_ref, resid_ref, up_ref,
    spread_ref,
    gains_out, qraw_out, kvraw_out, q_out, k_out, v_out, probs_out, mixed_out,
    layer_out, dres_out, dattn_out, away_out, sums_out, z_s, dg_s, du_s, rows_t_out, ff_t_out,
    attn_t_out, gate_s, upp_s, watt, sems, wff, ff_sems,
):
    attend_copies = fetch(gathered, watt, sems, 0, ATT)
    copies = fetch(gathered, wff, ff_sems, ATT, FFC)
    for copy in attend_copies:
        copy.wait()
    gains = cut(watt, 0, 640, 128).astype(F32).T
    gains_out[0:8] = gains[0:8]
    head_gains = dot(gains.astype(BF), heads_ref[...], 1, 0)
    gains_out[8:16] = jnp.concatenate([head_gains[0:8]] * 3, axis=1)
    query_gains, key_gains = head_gains[4:5], head_gains[5:6]
    rows = (normed_ref[...] * gains[0:1]).astype(BF)
    kv_raw = dot(rows, kv_weights(watt), 1, 0)
    kvraw_out[...] = kv_raw[:, :HD]
    key_norm, _ = norm_of(kv_raw[:, :HD], HD)
    key = rotate(key_norm * key_gains, cosine_ref[...], sine_ref[...]).astype(BF)
    value = kv_raw[:, HD:].astype(BF)
    k_out[...] = key
    v_out[...] = value
    rows_own = rows[2 * ROWS :]
    cosine, sine = cosine_ref[2 * ROWS :], sine_ref[2 * ROWS :]
    attn = jnp.zeros((ROWS, DP), F32)
    for head in range(HQ):
        at = slice(head * HD, (head + 1) * HD)
        query_raw = dot(rows_own, cut(watt, head, 0, 256), 1, 0)
        qraw_out[:, at] = query_raw
        query_norm, _ = norm_of(query_raw, HD)
        query = rotate(query_norm * query_gains, cosine, sine).astype(BF)
        q_out[:, at] = query
        scores = dot(query, key, 1, 1) * SCALE + bias_ref[...]
        exponent = jnp.exp(scores - jnp.max(scores, axis=-1, keepdims=True))
        probs = exponent * (1.0 / jnp.sum(exponent, axis=-1, keepdims=True))
        probs = probs.astype(BF)
        probs_out[head] = probs
        mixed = dot(probs, value, 1, 0).astype(BF)
        mixed_out[:, at] = mixed
        attn = attn + dot(mixed, cut(watt, head, 256, 256), 1, 1)
    attn_gains, ffin_gains, ffout_gains = gains[1:2], gains[2:3], gains[3:4]
    spread = spread_ref[...]
    upstream = up_ref[...]
    attn_normed, attn_inv = norm_of(attn, DM)
    mid = resid_ref[...] + attn_normed * attn_gains
    mid_normed, mid_inv = norm_of(mid, DM)
    rows = (mid_normed * ffin_gains).astype(BF)
    ff_sum = jnp.zeros((ROWS, DP), F32)
    for x in range(XS):
        at = slice(x * 512, (x + 1) * 512)
        copies[x].wait()
        gate = dot(rows, cut(wff, x, 0, 512), 1, 0)
        up = dot(rows, cut(wff, x, 512, 512), 1, 0)
        gate_s[:, at] = gate
        upp_s[:, at] = up
        act = 0.5 * gate * (1.0 + jnp.tanh(GELU_C * (gate + GELU_A * gate * gate * gate)))
        hidden = (act * up).astype(BF)
        z_s[:, at] = hidden
        ff_sum = ff_sum + dot(hidden, cut(wff, x, 1024, 512), 1, 1)
    ff_normed, ff_inv = norm_of(ff_sum, DM)
    layer = (mid + ff_normed * ffout_gains).astype(BF)
    layer_out[...] = dot(layer, spread, 1, 1).astype(BF)
    grad_gout = jnp.sum(upstream * ff_normed, axis=0, keepdims=True)
    grad_ff = norm_back(ff_normed, ff_inv, upstream * ffout_gains, DM).astype(BF)
    grad_mid = jnp.zeros((ROWS, DP), F32)
    for x in range(XS):
        at = slice(x * 512, (x + 1) * 512)
        grad_hidden = dot(grad_ff, cut(wff, x, 1024, 512), 1, 0)
        gate, up = gate_s[:, at], upp_s[:, at]
        curve = jnp.tanh(GELU_C * (gate + GELU_A * gate * gate * gate))
        slope = 0.5 * (1.0 + curve) + 0.5 * gate * (1.0 - curve * curve) * (
            GELU_C * (1.0 + 3.0 * GELU_A * gate * gate)
        )
        grad_gate = (grad_hidden * up * slope).astype(BF)
        grad_up = (grad_hidden * (0.5 * gate * (1.0 + curve))).astype(BF)
        dg_s[:, at] = grad_gate
        du_s[:, at] = grad_up
        grad_mid = grad_mid + dot(grad_gate, cut(wff, x, 0, 512), 1, 1)
        grad_mid = grad_mid + dot(grad_up, cut(wff, x, 512, 512), 1, 1)
    grad_gfin = jnp.sum(grad_mid * mid_normed, axis=0, keepdims=True)
    grad_resid = upstream + norm_back(mid_normed, mid_inv, grad_mid * ffin_gains, DM)
    dres_out[...] = grad_resid
    grad_gattn = jnp.sum(grad_resid * attn_normed, axis=0, keepdims=True)
    dattn_out[...] = norm_back(attn_normed, attn_inv, grad_resid * attn_gains, DM).astype(BF)
    zero = jnp.zeros((1, DP), F32)
    sums_out[...] = jnp.concatenate(
        [zero, grad_gattn, grad_gfin, grad_gout, zero, zero, zero, zero], axis=0
    )
    rows_t = dot(spread, rows, 1, 1).astype(BF)
    ff_t = dot(spread, grad_ff, 1, 1).astype(BF)
    attn_t = dot(spread, dattn_out[...], 1, 1).astype(BF)
    rows_t_out[...] = rows_t
    ff_t_out[...] = ff_t
    attn_t_out[...] = attn_t
    feed_half(1 - core_ref[0], away_out, rows_t, ff_t, attn_t, z_s, dg_s, du_s, mixed_out)


def feed_half(half, out, rows_t, ff_t, attn_t, z_ref, dg_ref, du_ref, mixed_ref):
    for x in range(XS):
        cols = pl.ds(pl.multiple_of(x * 512 + half * 256, 256), 256)
        for part, (lhs, rhs) in enumerate(((rows_t, dg_ref), (rows_t, du_ref), (ff_t, z_ref))):
            grad = dot(lhs, rhs[:, cols], 1, 0).astype(BF)
            out[x, :, part * 256 : (part + 1) * 256] = grad
        cols = pl.ds(pl.multiple_of(x * 256 + half * 128, 128), 128)
        out[x, :, 768:896] = dot(attn_t, mixed_ref[:, cols], 1, 0).astype(BF)


def feed_keep_kernel(
    core_ref, z_ref, dg_ref, du_ref, rows_t_ref, ff_t_ref, attn_t_ref, mixed_ref, keep_out
):
    feed_half(
        core_ref[0], keep_out, rows_t_ref[...], ff_t_ref[...], attn_t_ref[...],
        z_ref, dg_ref, du_ref, mixed_ref,
    )


def attend_back_kernel(
    core_ref, gathered, dattn_ref, normed_ref, qraw_ref, kvraw_ref, q_ref, k_ref, v_ref,
    probs_ref, cosine_ref, sine_ref, gains_ref, sums_ref, spread_ref, heads_ref,
    keep_out, away_out, dkv2_out, dkv1_out, dkv_out, part_out, wq_s, wkv_s, watt, sems,
):
    copies = fetch(gathered, watt, sems, 0, ATT)
    spread = spread_ref[...]
    query_gains, key_gains = gains_ref[12:13, :HD], gains_ref[13:14, :HD]
    grad_attn = dattn_ref[...]
    rows = (normed_ref[...] * gains_ref[0:1]).astype(BF)
    rows_t = dot(spread, rows, 1, 1).astype(BF)
    rows_own_t = rows_t[:, 2 * ROWS :]
    key, value = k_ref[...], v_ref[...]
    cosine, sine = cosine_ref[2 * ROWS :], sine_ref[2 * ROWS :]
    for copy in copies:
        copy.wait()
    grad_key = jnp.zeros((KEYS, HD), F32)
    grad_value = jnp.zeros((KEYS, HD), F32)
    part = jnp.zeros((ROWS, DP), F32)
    grad_gq = jnp.zeros((1, HD), F32)
    for head in range(HQ):
        at = slice(head * HD, (head + 1) * HD)
        grad_mixed = dot(grad_attn, cut(watt, head, 256, 256), 1, 0).astype(BF)
        probs_low = probs_ref[head]
        probs = probs_low.astype(F32)
        grad_value = grad_value + dot(probs_low, grad_mixed, 0, 0)
        grad_probs = dot(grad_mixed, value, 1, 1)
        grad_scores = (
            probs * (grad_probs - jnp.sum(probs * grad_probs, axis=-1, keepdims=True))
        ).astype(BF)
        grad_query = dot(grad_scores, key, 1, 0) * SCALE
        grad_key = grad_key + dot(grad_scores, q_ref[:, at], 0, 0)
        query_norm, query_inv = norm_of(qraw_ref[:, at], HD)
        grad_query = rotate(grad_query, cosine, -sine)
        grad_gq = grad_gq + jnp.sum(grad_query * query_norm, axis=0, keepdims=True)
        grad_raw = norm_back(query_norm, query_inv, grad_query * query_gains, HD).astype(BF)
        part = part + dot(grad_raw, cut(watt, head, 0, 256), 1, 1)
        wq_s[:, at] = dot(rows_own_t, grad_raw, 1, 0).astype(BF)
    part_out[...] = part
    key_norm, key_inv = norm_of(kvraw_ref[...], HD)
    grad_key = rotate(grad_key * SCALE, cosine_ref[...], -sine_ref[...])
    grad_gk = jnp.sum(grad_key * key_norm, axis=0, keepdims=True)
    grad_key = norm_back(key_norm, key_inv, grad_key * key_gains, HD)
    grad_kv = jnp.concatenate([grad_key, grad_value], axis=1).astype(BF)
    dkv2_out[...] = grad_kv[:ROWS]
    dkv1_out[...] = grad_kv[ROWS : 2 * ROWS]
    dkv_out[...] = grad_kv[2 * ROWS :]
    wkv_s[...] = dot(rows_t, grad_kv, 1, 0).astype(BF)
    kv_part = dot(grad_kv, kv_weights(watt), 1, 1)
    grad_gin = jnp.sum(kv_part * normed_ref[...], axis=0, keepdims=True)
    grad_gin = grad_gin + jnp.sum(part * normed_ref[2 * ROWS :], axis=0, keepdims=True)
    model = jnp.concatenate([grad_gin, sums_ref[1:8], jnp.zeros((120, DP), F32)], axis=0)
    zeros = jnp.zeros((1, HD), F32)
    heads = jnp.concatenate(
        [zeros, zeros, zeros, zeros, grad_gq, grad_gk, zeros, zeros, jnp.zeros((120, HD), F32)],
        axis=0,
    )
    gains = dot(spread, model.astype(BF), 1, 1) + dot(heads_ref[...], heads.astype(BF), 1, 1)
    gains = gains.astype(BF)
    core = core_ref[0]
    own_kv = jnp.broadcast_to(core, (DM, 128)) == 0
    for x in range(XS):
        for out, half in ((keep_out, core), (away_out, 1 - core)):
            cols = pl.ds(pl.multiple_of(x * 256 + half * 128, 128), 128)
            out[:, x, :, 0:128] = wq_s[:, cols].astype(F32).reshape(16, 40, 128).astype(BF)
        kv = wkv_s[:, x * 128 : (x + 1) * 128].astype(F32)
        kept = jnp.where(own_kv, kv, gains.astype(F32)).reshape(16, 40, 128).astype(BF)
        sent = jnp.where(own_kv, gains.astype(F32), kv).reshape(16, 40, 128).astype(BF)
        keep_out[:, x, :, 128:256] = kept
        away_out[:, x, :, 128:256] = sent


def final_kernel(core_ref, total_ref, other_ref, wq, wo, wg, wu, wd, wk, wv, *gain_refs):
    first = jnp.broadcast_to(core_ref[0], (OWN, total_ref.shape[1])) == 0
    mine = jnp.where(first, total_ref[0:OWN], total_ref[OWN : 2 * OWN])
    other = other_ref[...]
    left = jnp.where(first, mine, other)
    right = jnp.where(first, other, mine)
    for ref, at, size in ((wg, 0, 256), (wu, 256, 256), (wd, 512, 256), (wo, 768, 128), (wq, 896, 128)):
        ref[:, :size] = left[:, at : at + size]
        ref[:, size:] = right[:, at : at + size]
    wk[...] = left[:, 1152:1408]
    wv[...] = left[:, 1408:1664]
    gains = jnp.concatenate([right[:, 1024:1152], jnp.zeros((PAD - OWN, 128), F32)], axis=0).T
    for row, ref in enumerate(gain_refs):
        ref[...] = gains[row : row + 1, : ref.shape[1]]


def call(kernel, outs, args, scratch=(), word=None, weights=None, flops=0, vmem=0):
    whole = pl.BlockSpec(memory_space=pltpu.VMEM)
    first, first_specs = [], []
    if word is not None:
        first, first_specs = [word], [pl.BlockSpec(memory_space=pltpu.SMEM)]
    shapes = [pltpu.VMEM(shape, kind) for shape, kind in scratch]
    if weights is not None:
        gathered, *sizes = weights
        first, first_specs = first + [gathered], first_specs + [pl.BlockSpec(memory_space=pl.ANY)]
        for size in sizes:
            shapes += [pltpu.VMEM((XS, DPS, PAD, size), BF), pltpu.SemaphoreType.DMA((XS,))]
    return pl.pallas_call(
        kernel,
        out_shape=[jax.ShapeDtypeStruct(shape, kind) for shape, kind in outs],
        in_specs=first_specs + [whole] * len(args),
        out_specs=[whole] * len(outs),
        scratch_shapes=shapes,
        compiler_params=pltpu.CompilerParams(vmem_limit_bytes=vmem * 2**20),
        cost_estimate=pl.CostEstimate(flops=flops, bytes_accessed=20 * 2**20, transcendentals=0),
    )(*first, *args)


def per_device(
    hidden_in,
    out_grad,
    segment_ids,
    gain_input,
    w_query,
    w_key,
    w_value,
    gain_query,
    gain_key,
    w_out,
    gain_attn,
    gain_ffin,
    w_gate,
    w_up,
    w_down,
    gain_ffout,
):
    at = lax.axis_index("x")
    core = lax.axis_index("core")

    gains_own = jnp.zeros((128, 128), F32)
    for row, gain in enumerate(
        (gain_input, gain_attn, gain_ffin, gain_ffout, gain_query, gain_key)
    ):
        size = gain.shape[0]
        gains_own = gains_own + jnp.pad(
            gain.astype(F32)[None], ((row, 127 - row), (0, 128 - size))
        )
    width = ATT + FFC
    at_word = at.astype(jnp.int32).reshape(1)
    whole = pl.BlockSpec(memory_space=pltpu.VMEM)
    packed = pl.pallas_call(
        pack_kernel,
        out_shape=jax.ShapeDtypeStruct((PAD, width), BF),
        in_specs=[whole] * 7 + [pl.BlockSpec(memory_space=pltpu.SMEM)],
        out_specs=whole,
    )(jnp.concatenate([w_query[:, 0], w_out[:, 0]], axis=1), w_gate, w_up, w_down, w_key, w_value, gains_own, at_word)
    gathered = lax.all_gather(packed, EVERY, axis=0, tiled=False).reshape(DPS, XS, PAD, width)

    before_one = lax.ppermute(hidden_in, "x", [(i, i + 1) for i in range(XS - 1)])
    before_two = lax.ppermute(hidden_in, "x", [(i, i + 2) for i in range(XS - 2)])
    rows_low = jnp.concatenate([before_two, before_one, hidden_in], axis=0)
    spread = spread_matrix()
    resid_all = dot(rows_low, spread, 1, 0)
    upstream = dot(out_grad, spread, 1, 0)
    normed_all, inverse_all = norm_of(resid_all, DM)
    resid_in = resid_all[2 * ROWS :]

    offsets = jnp.arange(segment_ids.shape[0], dtype=jnp.int32)
    live = segment_ids >= 0
    tail_start = jnp.sum(live.astype(jnp.int32))
    positions = offsets - jnp.where(live, segment_ids, tail_start)
    positions = jnp.concatenate([jnp.zeros((2 * ROWS,), jnp.int32), positions], axis=0)
    positions = lax.dynamic_slice_in_dim(positions, at * ROWS, KEYS, 0)
    frequency = ROPE_BASE ** (-2.0 * jnp.arange(HALF, dtype=F32) / HD)
    angles = positions.astype(F32)[:, None] * frequency[None, :]
    cosine, sine = jnp.cos(angles), jnp.sin(angles)
    ids = jnp.concatenate([jnp.full((2 * ROWS,), -2, jnp.int32), segment_ids], axis=0)
    key_ids = lax.dynamic_slice_in_dim(ids, at * ROWS, KEYS, 0)
    query_ids = key_ids[2 * ROWS :]
    row_at = lax.broadcasted_iota(jnp.int32, (ROWS, KEYS), 0)
    col_at = lax.broadcasted_iota(jnp.int32, (ROWS, KEYS), 1)
    gap = row_at + 2 * ROWS - col_at
    visible = (
        (query_ids[:, None] == key_ids[None, :])
        & (gap >= 0)
        & (gap < WINDOW)
        & ((query_ids[:, None] >= 0) | (gap == 0))
    )
    bias = jnp.where(visible, 0.0, NEGATIVE).astype(F32)

    core_word = core.astype(jnp.int32).reshape(1)
    head_rows = head_matrix(OWN)
    core_word, head_rows = lax.optimization_barrier((core_word, head_rows))
    (
        gains, query_raw, kv_raw, query, key, value, probs, mixed,
        layer_out, grad_resid, grad_attn, away_ff, sums, *feed,
    ) = call(
        forward_kernel,
        [
            ((16, DP), F32),
            ((ROWS, HQ * HD), F32),
            ((KEYS, HD), F32),
            ((ROWS, HQ * HD), BF),
            ((KEYS, HD), BF),
            ((KEYS, HD), BF),
            ((HQ, ROWS, KEYS), BF),
            ((ROWS, HQ * HD), BF),
            ((ROWS, DM), BF),
            ((ROWS, DP), F32),
            ((ROWS, DP), BF),
            ((XS, DM, 896), BF),
            ((8, DP), F32),
            ((ROWS, 2048), BF),
            ((ROWS, 2048), BF),
            ((ROWS, 2048), BF),
            ((DM, ROWS), BF),
            ((DM, ROWS), BF),
            ((DM, ROWS), BF),
        ],
        [normed_all, cosine, sine, bias, head_matrix(PAD), resid_in, upstream, spread],
        [((ROWS, 2048), F32), ((ROWS, 2048), F32)],
        word=core_word,
        weights=(gathered, ATT, FFC),
        flops=10**10,
        vmem=46,
    )
    swap = [(0, 1), (1, 0)]
    arrived_ff = lax.ppermute(away_ff, "core", swap)
    (keep_ff,) = call(
        feed_keep_kernel, [((XS, DM, 896), BF)], feed + [mixed], word=core_word, flops=2 * 10**9, vmem=20
    )
    both_ff = (keep_ff.astype(F32) + arrived_ff.astype(F32)).astype(BF)
    both_ff, grad_attn = lax.optimization_barrier((both_ff, grad_attn))
    column_ff = lax.psum_scatter(
        both_ff.reshape(XS * DM, 896), "x", scatter_dimension=0, tiled=True
    )
    keep_att, away_att, grad_kv_two, grad_kv_one, grad_kv, query_part = call(
        attend_back_kernel,
        [
            ((16, XS, 40, 256), BF),
            ((16, XS, 40, 256), BF),
            ((ROWS, 2 * HD), BF),
            ((ROWS, 2 * HD), BF),
            ((ROWS, 2 * HD), BF),
            ((ROWS, DP), F32),
        ],
        [
            grad_attn, normed_all, query_raw, kv_raw, query, key, value, probs,
            cosine, sine, gains, sums, spread, head_rows,
        ],
        [((DM, 1024), BF), ((DM, 512), BF)],
        word=core_word,
        weights=(gathered, ATT),
        flops=4 * 10**9,
        vmem=60,
    )
    arrived_att = lax.ppermute(away_att, "core", swap)
    from_one = lax.ppermute(
        grad_kv_one, "x", [(i + 1, i) for i in range(XS - 1)]
    )
    from_two = lax.ppermute(grad_kv_two, "x", [(i + 2, i) for i in range(XS - 2)])
    both_att = (keep_att.astype(F32) + arrived_att.astype(F32)).astype(BF)
    parts_att = lax.all_to_all(both_att.reshape(16, 160, 256), ("z", "y"), 0, 0, tiled=True)
    parts_att, column_ff = lax.optimization_barrier((parts_att, column_ff))
    row_att = jnp.sum(parts_att.astype(F32), axis=0).astype(BF)
    one, two, three = (
        lax.ppermute(row_att, "x", [(i, (i + step) % XS) for i in range(XS)]).astype(F32)
        for step in (1, 2, 3)
    )
    all_att = ((row_att.astype(F32) + two) + (one + three)).reshape(XS, 40, 256)
    total_att = lax.dynamic_index_in_dim(all_att, at, 0, keepdims=False)
    total_kv = all_att[:, :, 128:].transpose(1, 0, 2).reshape(40, 512)
    parts_ff = lax.all_to_all(column_ff.reshape(16, 40, 896), ("z", "y"), 0, 0, tiled=True)
    total_ff = jnp.sum(parts_ff.astype(F32), axis=0)
    total = jnp.concatenate([total_ff, total_att, total_kv], axis=1)

    grad_kv_own = (
        grad_kv.astype(F32) + from_one.astype(F32) + from_two.astype(F32)
    ).astype(BF)
    kv_cols = gathered[:, :, :, 512:640].transpose(0, 2, 1, 3).reshape(DP, 2 * HD)
    grad_in = query_part + dot(grad_kv_own, kv_cols, 1, 1)
    normed_in, inverse_in = normed_all[2 * ROWS :], inverse_all[2 * ROWS :]
    input_grad = grad_resid + norm_back(normed_in, inverse_in, grad_in * gains[0:1], DM)
    grad_top = input_grad.astype(BF)
    grad_rest = (input_grad - grad_top.astype(F32)).astype(BF)
    input_grad = dot(grad_top, spread, 1, 1) + dot(grad_rest, spread, 1, 1)

    other = lax.ppermute(lax.dynamic_slice_in_dim(total, (1 - core) * OWN, OWN, 0), "core", swap)
    outs = [(OWN, 256), (OWN, 256), (OWN, 512), (OWN, 512), (OWN, 512), (OWN, 256), (OWN, 256)]
    outs += [(1, OWN)] * 4 + [(1, 8)] * 2
    grad_wq, grad_wo, grad_wg, grad_wu, grad_wd, grad_wk, grad_wv, *grad_gains = call(
        final_kernel, [(shape, F32) for shape in outs], [total, other], word=core_word, vmem=16
    )
    grad_gains = [grad[0] for grad in grad_gains]
    return (
        layer_out,
        input_grad,
        grad_gains[0],
        grad_wq[:, None, :],
        grad_wk,
        grad_wv,
        grad_gains[4],
        grad_gains[5],
        grad_wo[:, None, :],
        grad_gains[1],
        grad_gains[2],
        grad_wg,
        grad_wu,
        grad_wd,
        grad_gains[3],
    )


def solution(mesh):
    fine = Mesh(mesh.devices.reshape(ZS, YS, CS, XS), EVERY)
    dp = ("z", "y", "core")
    in_specs = (
        P(EVERY, None),
        P(EVERY, None),
        P(dp),
        P(dp),
        P(dp, "x", None),
        P(dp, None),
        P(dp, None),
        P(dp),
        P(dp),
        P(dp, "x", None),
        P(dp),
        P(dp),
        P(dp, "x"),
        P(dp, "x"),
        P(dp, "x"),
        P(dp),
    )
    out_specs = (
        P(EVERY, None),
        P(EVERY, None),
        P(dp),
        P(dp, "x", None),
        P(dp, None),
        P(dp, None),
        P(dp),
        P(dp),
        P(dp, "x", None),
        P(dp),
        P(dp),
        P(dp, "x"),
        P(dp, "x"),
        P(dp, "x"),
        P(dp),
    )
    return jax.shard_map(
        per_device, mesh=fine, in_specs=in_specs, out_specs=out_specs, check_vma=False
    )
```

```python
import jax
import jax.numpy as jnp
from jax import lax
from jax.experimental import pallas as pl
from jax.experimental.pallas import tpu as pltpu
from jax.sharding import Mesh, PartitionSpec as P

WINDOW = 512
EPS = 1e-06
ROPE_BASE = 10000.0
NEGATIVE = -1e30
ZS, YS, CS, XS = 4, 4, 2, 4
CHIP = ("z", "y", "x")
EVERY = ("z", "y", "core", "x")
DPS = 32
OWN = 20
PAD = 24
DM = 640
DP = DPS * PAD
ROWS = 256
KEYS = 3 * ROWS
HQ = 4
HD = 256
HALF = HD // 2
ATT = 768
FFC = 1536
SCALE = HD**-0.5
GELU_C = 0.7978845608028654
GELU_A = 0.044715
BF = jnp.bfloat16
F32 = jnp.float32


def norm_of(values_in, width):
    inverse = lax.rsqrt(
        jnp.sum(values_in * values_in, axis=-1, keepdims=True) * (1.0 / width) + EPS
    )
    return values_in * inverse, inverse


def norm_back(normed, inverse, upstream, width):
    mean = jnp.sum(upstream * normed, axis=-1, keepdims=True) * (1.0 / width)
    return inverse * (upstream - normed * mean)


def rotate(values_in, cosine, sine):
    first, second = values_in[:, :HALF], values_in[:, HALF:]
    return jnp.concatenate(
        [first * cosine - second * sine, second * cosine + first * sine], axis=1
    )


def dot(lhs, rhs, lhs_dim, rhs_dim):
    return lax.dot_general(
        lhs, rhs, (((lhs_dim,), (rhs_dim,)), ((), ())), preferred_element_type=F32
    )


def spread_matrix():
    row = lax.broadcasted_iota(jnp.int32, (DM, DP), 0)
    col = lax.broadcasted_iota(jnp.int32, (DM, DP), 1)
    return ((col % PAD < OWN) & (row == (col // PAD) * OWN + col % PAD)).astype(BF)


def head_matrix(step):
    row = lax.broadcasted_iota(jnp.int32, (DPS * step, HD), 0)
    col = lax.broadcasted_iota(jnp.int32, (DPS * step, HD), 1)
    return ((row // step == col // 8) & (row % step == col % 8)).astype(BF)


def fetch(gathered, held, sems, first, size):
    copies = [
        pltpu.make_async_copy(gathered.at[:, x, :, first : first + size], held.at[x], sems.at[x])
        for x in range(XS)
    ]
    for copy in copies:
        copy.start()
    return copies


def cut(held, x, first, size):
    return held[x, :, :, first : first + size].reshape(DP, size)


def kv_weights(watt):
    return jnp.concatenate([cut(watt, x, 512, 128) for x in range(XS)], axis=1)


def pack_kernel(wqo_ref, wg_ref, wu_ref, wd_ref, wk_ref, wv_ref, gains_ref, at_ref, out):
    out[...] = jnp.zeros(out.shape, BF)
    out[0:OWN, 0:512] = wqo_ref[...]
    at = at_ref[0]
    kv = jnp.where(
        jnp.broadcast_to(at, (OWN, 256)) < 2, wk_ref[...].astype(F32), wv_ref[...].astype(F32)
    )
    kv = jnp.where(jnp.broadcast_to(at % 2, (OWN, 128)) == 0, kv[:, :128], kv[:, 128:])
    out[0:OWN, 512:640] = kv.astype(BF)
    out[:, 640:768] = gains_ref[...].T[:PAD].astype(BF)
    out[0:OWN, 768:1280] = wg_ref[...]
    out[0:OWN, 1280:1792] = wu_ref[...]
    out[0:OWN, 1792:2304] = wd_ref[...]


def forward_kernel(
    core_ref, gathered, normed_ref, cosine_ref, sine_ref, bias_ref, heads_ref, resid_ref, up_ref,
    spread_ref,
    gains_out, qraw_out, kvraw_out, q_out, k_out, v_out, probs_out, mixed_out,
    layer_out, dres_out, dattn_out, away_out, sums_out, z_s, dg_s, du_s, rows_t_out, ff_t_out,
    attn_t_out, gate_s, upp_s, watt, sems, wff, ff_sems,
):
    attend_copies = fetch(gathered, watt, sems, 0, ATT)
    copies = fetch(gathered, wff, ff_sems, ATT, FFC)
    for copy in attend_copies:
        copy.wait()
    gains = cut(watt, 0, 640, 128).astype(F32).T
    gains_out[0:8] = gains[0:8]
    head_gains = dot(gains.astype(BF), heads_ref[...], 1, 0)
    gains_out[8:16] = jnp.concatenate([head_gains[0:8]] * 3, axis=1)
    query_gains, key_gains = head_gains[4:5], head_gains[5:6]
    rows = (normed_ref[...] * gains[0:1]).astype(BF)
    kv_raw = dot(rows, kv_weights(watt), 1, 0)
    kvraw_out[...] = kv_raw[:, :HD]
    key_norm, _ = norm_of(kv_raw[:, :HD], HD)
    key = rotate(key_norm * key_gains, cosine_ref[...], sine_ref[...]).astype(BF)
    value = kv_raw[:, HD:].astype(BF)
    k_out[...] = key
    v_out[...] = value
    rows_own = rows[2 * ROWS :]
    cosine, sine = cosine_ref[2 * ROWS :], sine_ref[2 * ROWS :]
    attn = jnp.zeros((ROWS, DP), F32)
    for head in range(HQ):
        at = slice(head * HD, (head + 1) * HD)
        query_raw = dot(rows_own, cut(watt, head, 0, 256), 1, 0)
        qraw_out[:, at] = query_raw
        query_norm, _ = norm_of(query_raw, HD)
        query = rotate(query_norm * query_gains, cosine, sine).astype(BF)
        q_out[:, at] = query
        scores = dot(query, key, 1, 1) * SCALE + bias_ref[...]
        exponent = jnp.exp(scores - jnp.max(scores, axis=-1, keepdims=True))
        probs = exponent * (1.0 / jnp.sum(exponent, axis=-1, keepdims=True))
        probs = probs.astype(BF)
        probs_out[head] = probs
        mixed = dot(probs, value, 1, 0).astype(BF)
        mixed_out[:, at] = mixed
        attn = attn + dot(mixed, cut(watt, head, 256, 256), 1, 1)
    attn_gains, ffin_gains, ffout_gains = gains[1:2], gains[2:3], gains[3:4]
    spread = spread_ref[...]
    upstream = up_ref[...]
    attn_normed, attn_inv = norm_of(attn, DM)
    mid = resid_ref[...] + attn_normed * attn_gains
    mid_normed, mid_inv = norm_of(mid, DM)
    rows = (mid_normed * ffin_gains).astype(BF)
    ff_sum = jnp.zeros((ROWS, DP), F32)
    for x in range(XS):
        at = slice(x * 512, (x + 1) * 512)
        copies[x].wait()
        gate = dot(rows, cut(wff, x, 0, 512), 1, 0)
        up = dot(rows, cut(wff, x, 512, 512), 1, 0)
        gate_s[:, at] = gate
        upp_s[:, at] = up
        act = 0.5 * gate * (1.0 + jnp.tanh(GELU_C * (gate + GELU_A * gate * gate * gate)))
        hidden = (act * up).astype(BF)
        z_s[:, at] = hidden
        ff_sum = ff_sum + dot(hidden, cut(wff, x, 1024, 512), 1, 1)
    ff_normed, ff_inv = norm_of(ff_sum, DM)
    layer = (mid + ff_normed * ffout_gains).astype(BF)
    layer_out[...] = dot(layer, spread, 1, 1).astype(BF)
    grad_gout = jnp.sum(upstream * ff_normed, axis=0, keepdims=True)
    grad_ff = norm_back(ff_normed, ff_inv, upstream * ffout_gains, DM).astype(BF)
    grad_mid = jnp.zeros((ROWS, DP), F32)
    for x in range(XS):
        at = slice(x * 512, (x + 1) * 512)
        grad_hidden = dot(grad_ff, cut(wff, x, 1024, 512), 1, 0)
        gate, up = gate_s[:, at], upp_s[:, at]
        curve = jnp.tanh(GELU_C * (gate + GELU_A * gate * gate * gate))
        slope = 0.5 * (1.0 + curve) + 0.5 * gate * (1.0 - curve * curve) * (
            GELU_C * (1.0 + 3.0 * GELU_A * gate * gate)
        )
        grad_gate = (grad_hidden * up * slope).astype(BF)
        grad_up = (grad_hidden * (0.5 * gate * (1.0 + curve))).astype(BF)
        dg_s[:, at] = grad_gate
        du_s[:, at] = grad_up
        grad_mid = grad_mid + dot(grad_gate, cut(wff, x, 0, 512), 1, 1)
        grad_mid = grad_mid + dot(grad_up, cut(wff, x, 512, 512), 1, 1)
    grad_gfin = jnp.sum(grad_mid * mid_normed, axis=0, keepdims=True)
    grad_resid = upstream + norm_back(mid_normed, mid_inv, grad_mid * ffin_gains, DM)
    dres_out[...] = grad_resid
    grad_gattn = jnp.sum(grad_resid * attn_normed, axis=0, keepdims=True)
    dattn_out[...] = norm_back(attn_normed, attn_inv, grad_resid * attn_gains, DM).astype(BF)
    zero = jnp.zeros((1, DP), F32)
    sums_out[...] = jnp.concatenate(
        [zero, grad_gattn, grad_gfin, grad_gout, zero, zero, zero, zero], axis=0
    )
    rows_t = dot(spread, rows, 1, 1).astype(BF)
    ff_t = dot(spread, grad_ff, 1, 1).astype(BF)
    attn_t = dot(spread, dattn_out[...], 1, 1).astype(BF)
    rows_t_out[...] = rows_t
    ff_t_out[...] = ff_t
    attn_t_out[...] = attn_t
    feed_half(1 - core_ref[0], away_out, rows_t, ff_t, attn_t, z_s, dg_s, du_s, mixed_out)


def feed_half(half, out, rows_t, ff_t, attn_t, z_ref, dg_ref, du_ref, mixed_ref):
    for x in range(XS):
        cols = pl.ds(pl.multiple_of(x * 512 + half * 256, 256), 256)
        for part, (lhs, rhs) in enumerate(((rows_t, dg_ref), (rows_t, du_ref), (ff_t, z_ref))):
            grad = dot(lhs, rhs[:, cols], 1, 0).astype(BF)
            out[x, :, part * 256 : (part + 1) * 256] = grad
        cols = pl.ds(pl.multiple_of(x * 256 + half * 128, 128), 128)
        out[x, :, 768:896] = dot(attn_t, mixed_ref[:, cols], 1, 0).astype(BF)


def feed_keep_kernel(
    core_ref, z_ref, dg_ref, du_ref, rows_t_ref, ff_t_ref, attn_t_ref, mixed_ref, keep_out
):
    feed_half(
        core_ref[0], keep_out, rows_t_ref[...], ff_t_ref[...], attn_t_ref[...],
        z_ref, dg_ref, du_ref, mixed_ref,
    )


def attend_back_kernel(
    core_ref, gathered, dattn_ref, normed_ref, qraw_ref, kvraw_ref, q_ref, k_ref, v_ref,
    probs_ref, cosine_ref, sine_ref, gains_ref, sums_ref, spread_ref, heads_ref,
    keep_out, away_out, dkv2_out, dkv1_out, dkv_out, part_out, wq_s, wkv_s, watt, sems,
):
    copies = fetch(gathered, watt, sems, 0, ATT)
    spread = spread_ref[...]
    query_gains, key_gains = gains_ref[12:13, :HD], gains_ref[13:14, :HD]
    grad_attn = dattn_ref[...]
    rows = (normed_ref[...] * gains_ref[0:1]).astype(BF)
    rows_t = dot(spread, rows, 1, 1).astype(BF)
    rows_own_t = rows_t[:, 2 * ROWS :]
    key, value = k_ref[...], v_ref[...]
    cosine, sine = cosine_ref[2 * ROWS :], sine_ref[2 * ROWS :]
    for copy in copies:
        copy.wait()
    grad_key = jnp.zeros((KEYS, HD), F32)
    grad_value = jnp.zeros((KEYS, HD), F32)
    part = jnp.zeros((ROWS, DP), F32)
    grad_gq = jnp.zeros((1, HD), F32)
    for head in range(HQ):
        at = slice(head * HD, (head + 1) * HD)
        grad_mixed = dot(grad_attn, cut(watt, head, 256, 256), 1, 0).astype(BF)
        probs_low = probs_ref[head]
        probs = probs_low.astype(F32)
        grad_value = grad_value + dot(probs_low, grad_mixed, 0, 0)
        grad_probs = dot(grad_mixed, value, 1, 1)
        grad_scores = (
            probs * (grad_probs - jnp.sum(probs * grad_probs, axis=-1, keepdims=True))
        ).astype(BF)
        grad_query = dot(grad_scores, key, 1, 0) * SCALE
        grad_key = grad_key + dot(grad_scores, q_ref[:, at], 0, 0)
        query_norm, query_inv = norm_of(qraw_ref[:, at], HD)
        grad_query = rotate(grad_query, cosine, -sine)
        grad_gq = grad_gq + jnp.sum(grad_query * query_norm, axis=0, keepdims=True)
        grad_raw = norm_back(query_norm, query_inv, grad_query * query_gains, HD).astype(BF)
        part = part + dot(grad_raw, cut(watt, head, 0, 256), 1, 1)
        wq_s[:, at] = dot(rows_own_t, grad_raw, 1, 0).astype(BF)
    part_out[...] = part
    key_norm, key_inv = norm_of(kvraw_ref[...], HD)
    grad_key = rotate(grad_key * SCALE, cosine_ref[...], -sine_ref[...])
    grad_gk = jnp.sum(grad_key * key_norm, axis=0, keepdims=True)
    grad_key = norm_back(key_norm, key_inv, grad_key * key_gains, HD)
    grad_kv = jnp.concatenate([grad_key, grad_value], axis=1).astype(BF)
    dkv2_out[...] = grad_kv[:ROWS]
    dkv1_out[...] = grad_kv[ROWS : 2 * ROWS]
    dkv_out[...] = grad_kv[2 * ROWS :]
    wkv_s[...] = dot(rows_t, grad_kv, 1, 0).astype(BF)
    kv_part = dot(grad_kv, kv_weights(watt), 1, 1)
    grad_gin = jnp.sum(kv_part * normed_ref[...], axis=0, keepdims=True)
    grad_gin = grad_gin + jnp.sum(part * normed_ref[2 * ROWS :], axis=0, keepdims=True)
    model = jnp.concatenate([grad_gin, sums_ref[1:8], jnp.zeros((120, DP), F32)], axis=0)
    zeros = jnp.zeros((1, HD), F32)
    heads = jnp.concatenate(
        [zeros, zeros, zeros, zeros, grad_gq, grad_gk, zeros, zeros, jnp.zeros((120, HD), F32)],
        axis=0,
    )
    gains = dot(spread, model.astype(BF), 1, 1) + dot(heads_ref[...], heads.astype(BF), 1, 1)
    gains = gains.astype(BF)
    core = core_ref[0]
    own_kv = jnp.broadcast_to(core, (DM, 128)) == 0
    for x in range(XS):
        for out, half in ((keep_out, core), (away_out, 1 - core)):
            cols = pl.ds(pl.multiple_of(x * 256 + half * 128, 128), 128)
            out[:, x, :, 0:128] = wq_s[:, cols].astype(F32).reshape(16, 40, 128).astype(BF)
        kv = wkv_s[:, x * 128 : (x + 1) * 128].astype(F32)
        kept = jnp.where(own_kv, kv, gains.astype(F32)).reshape(16, 40, 128).astype(BF)
        sent = jnp.where(own_kv, gains.astype(F32), kv).reshape(16, 40, 128).astype(BF)
        keep_out[:, x, :, 128:256] = kept
        away_out[:, x, :, 128:256] = sent


def final_kernel(core_ref, total_ref, other_ref, wq, wo, wg, wu, wd, wk, wv, *gain_refs):
    first = jnp.broadcast_to(core_ref[0], (OWN, total_ref.shape[1])) == 0
    mine = jnp.where(first, total_ref[0:OWN], total_ref[OWN : 2 * OWN])
    other = other_ref[...]
    left = jnp.where(first, mine, other)
    right = jnp.where(first, other, mine)
    for ref, at, size in ((wg, 0, 256), (wu, 256, 256), (wd, 512, 256), (wo, 768, 128), (wq, 896, 128)):
        ref[:, :size] = left[:, at : at + size]
        ref[:, size:] = right[:, at : at + size]
    wk[...] = left[:, 1152:1408]
    wv[...] = left[:, 1408:1664]
    gains = jnp.concatenate([right[:, 1024:1152], jnp.zeros((PAD - OWN, 128), F32)], axis=0).T
    for row, ref in enumerate(gain_refs):
        ref[...] = gains[row : row + 1, : ref.shape[1]]


def call(kernel, outs, args, scratch=(), word=None, weights=None, flops=0, vmem=0):
    whole = pl.BlockSpec(memory_space=pltpu.VMEM)
    first, first_specs = [], []
    if word is not None:
        first, first_specs = [word], [pl.BlockSpec(memory_space=pltpu.SMEM)]
    shapes = [pltpu.VMEM(shape, kind) for shape, kind in scratch]
    if weights is not None:
        gathered, *sizes = weights
        first, first_specs = first + [gathered], first_specs + [pl.BlockSpec(memory_space=pl.ANY)]
        for size in sizes:
            shapes += [pltpu.VMEM((XS, DPS, PAD, size), BF), pltpu.SemaphoreType.DMA((XS,))]
    return pl.pallas_call(
        kernel,
        out_shape=[jax.ShapeDtypeStruct(shape, kind) for shape, kind in outs],
        in_specs=first_specs + [whole] * len(args),
        out_specs=[whole] * len(outs),
        scratch_shapes=shapes,
        compiler_params=pltpu.CompilerParams(vmem_limit_bytes=vmem * 2**20),
        cost_estimate=pl.CostEstimate(flops=flops, bytes_accessed=20 * 2**20, transcendentals=0),
    )(*first, *args)


def per_device(
    hidden_in,
    out_grad,
    segment_ids,
    gain_input,
    w_query,
    w_key,
    w_value,
    gain_query,
    gain_key,
    w_out,
    gain_attn,
    gain_ffin,
    w_gate,
    w_up,
    w_down,
    gain_ffout,
):
    at = lax.axis_index("x")
    core = lax.axis_index("core")

    gains_own = jnp.zeros((128, 128), F32)
    for row, gain in enumerate(
        (gain_input, gain_attn, gain_ffin, gain_ffout, gain_query, gain_key)
    ):
        size = gain.shape[0]
        gains_own = gains_own + jnp.pad(
            gain.astype(F32)[None], ((row, 127 - row), (0, 128 - size))
        )
    width = ATT + FFC
    at_word = at.astype(jnp.int32).reshape(1)
    whole = pl.BlockSpec(memory_space=pltpu.VMEM)
    packed = pl.pallas_call(
        pack_kernel,
        out_shape=jax.ShapeDtypeStruct((PAD, width), BF),
        in_specs=[whole] * 7 + [pl.BlockSpec(memory_space=pltpu.SMEM)],
        out_specs=whole,
    )(jnp.concatenate([w_query[:, 0], w_out[:, 0]], axis=1), w_gate, w_up, w_down, w_key, w_value, gains_own, at_word)
    gathered = lax.all_gather(packed, EVERY, axis=0, tiled=False).reshape(DPS, XS, PAD, width)

    before_one = lax.ppermute(hidden_in, "x", [(i, i + 1) for i in range(XS - 1)])
    before_two = lax.ppermute(hidden_in, "x", [(i, i + 2) for i in range(XS - 2)])
    rows_low = jnp.concatenate([before_two, before_one, hidden_in], axis=0)
    spread = spread_matrix()
    resid_all = dot(rows_low, spread, 1, 0)
    upstream = dot(out_grad, spread, 1, 0)
    normed_all, inverse_all = norm_of(resid_all, DM)
    resid_in = resid_all[2 * ROWS :]

    offsets = jnp.arange(segment_ids.shape[0], dtype=jnp.int32)
    live = segment_ids >= 0
    tail_start = jnp.sum(live.astype(jnp.int32))
    positions = offsets - jnp.where(live, segment_ids, tail_start)
    positions = jnp.concatenate([jnp.zeros((2 * ROWS,), jnp.int32), positions], axis=0)
    positions = lax.dynamic_slice_in_dim(positions, at * ROWS, KEYS, 0)
    frequency = ROPE_BASE ** (-2.0 * jnp.arange(HALF, dtype=F32) / HD)
    angles = positions.astype(F32)[:, None] * frequency[None, :]
    cosine, sine = jnp.cos(angles), jnp.sin(angles)
    ids = jnp.concatenate([jnp.full((2 * ROWS,), -2, jnp.int32), segment_ids], axis=0)
    key_ids = lax.dynamic_slice_in_dim(ids, at * ROWS, KEYS, 0)
    query_ids = key_ids[2 * ROWS :]
    row_at = lax.broadcasted_iota(jnp.int32, (ROWS, KEYS), 0)
    col_at = lax.broadcasted_iota(jnp.int32, (ROWS, KEYS), 1)
    gap = row_at + 2 * ROWS - col_at
    visible = (
        (query_ids[:, None] == key_ids[None, :])
        & (gap >= 0)
        & (gap < WINDOW)
        & ((query_ids[:, None] >= 0) | (gap == 0))
    )
    bias = jnp.where(visible, 0.0, NEGATIVE).astype(F32)

    core_word = core.astype(jnp.int32).reshape(1)
    head_rows = head_matrix(OWN)
    core_word, head_rows = lax.optimization_barrier((core_word, head_rows))
    (
        gains, query_raw, kv_raw, query, key, value, probs, mixed,
        layer_out, grad_resid, grad_attn, away_ff, sums, *feed,
    ) = call(
        forward_kernel,
        [
            ((16, DP), F32),
            ((ROWS, HQ * HD), F32),
            ((KEYS, HD), F32),
            ((ROWS, HQ * HD), BF),
            ((KEYS, HD), BF),
            ((KEYS, HD), BF),
            ((HQ, ROWS, KEYS), BF),
            ((ROWS, HQ * HD), BF),
            ((ROWS, DM), BF),
            ((ROWS, DP), F32),
            ((ROWS, DP), BF),
            ((XS, DM, 896), BF),
            ((8, DP), F32),
            ((ROWS, 2048), BF),
            ((ROWS, 2048), BF),
            ((ROWS, 2048), BF),
            ((DM, ROWS), BF),
            ((DM, ROWS), BF),
            ((DM, ROWS), BF),
        ],
        [normed_all, cosine, sine, bias, head_matrix(PAD), resid_in, upstream, spread],
        [((ROWS, 2048), F32), ((ROWS, 2048), F32)],
        word=core_word,
        weights=(gathered, ATT, FFC),
        flops=10**10,
        vmem=50,
    )
    swap = [(0, 1), (1, 0)]
    arrived_ff = lax.ppermute(away_ff, "core", swap)
    (keep_ff,) = call(
        feed_keep_kernel, [((XS, DM, 896), BF)], feed + [mixed], word=core_word, flops=2 * 10**9, vmem=20
    )
    both_ff = (keep_ff.astype(F32) + arrived_ff.astype(F32)).astype(BF)
    both_ff, grad_attn = lax.optimization_barrier((both_ff, grad_attn))
    column_ff = lax.psum_scatter(
        both_ff.reshape(XS * DM, 896), "x", scatter_dimension=0, tiled=True
    )
    keep_att, away_att, grad_kv_two, grad_kv_one, grad_kv, query_part = call(
        attend_back_kernel,
        [
            ((16, XS, 40, 256), BF),
            ((16, XS, 40, 256), BF),
            ((ROWS, 2 * HD), BF),
            ((ROWS, 2 * HD), BF),
            ((ROWS, 2 * HD), BF),
            ((ROWS, DP), F32),
        ],
        [
            grad_attn, normed_all, query_raw, kv_raw, query, key, value, probs,
            cosine, sine, gains, sums, spread, head_rows,
        ],
        [((DM, 1024), BF), ((DM, 512), BF)],
        word=core_word,
        weights=(gathered, ATT),
        flops=4 * 10**9,
        vmem=60,
    )
    arrived_att = lax.ppermute(away_att, "core", swap)
    from_one = lax.ppermute(
        grad_kv_one, "x", [(i + 1, i) for i in range(XS - 1)]
    )
    from_two = lax.ppermute(grad_kv_two, "x", [(i + 2, i) for i in range(XS - 2)])
    both_att = (keep_att.astype(F32) + arrived_att.astype(F32)).astype(BF)
    parts_att = lax.all_to_all(both_att.reshape(16, 160, 256), ("z", "y"), 0, 0, tiled=True)
    parts_att, column_ff = lax.optimization_barrier((parts_att, column_ff))
    row_att = jnp.sum(parts_att.astype(F32), axis=0).astype(BF)
    one, two, three = (
        lax.ppermute(row_att, "x", [(i, (i + step) % XS) for i in range(XS)]).astype(F32)
        for step in (1, 2, 3)
    )
    all_att = ((row_att.astype(F32) + two) + (one + three)).reshape(XS, 40, 256)
    total_att = lax.dynamic_index_in_dim(all_att, at, 0, keepdims=False)
    total_kv = all_att[:, :, 128:].transpose(1, 0, 2).reshape(40, 512)
    parts_ff = lax.all_to_all(column_ff.reshape(16, 40, 896), ("z", "y"), 0, 0, tiled=True)
    total_ff = jnp.sum(parts_ff.astype(F32), axis=0)
    total = jnp.concatenate([total_ff, total_att, total_kv], axis=1)

    grad_kv_own = (
        grad_kv.astype(F32) + from_one.astype(F32) + from_two.astype(F32)
    ).astype(BF)
    kv_cols = gathered[:, :, :, 512:640].transpose(0, 2, 1, 3).reshape(DP, 2 * HD)
    grad_in = query_part + dot(grad_kv_own, kv_cols, 1, 1)
    normed_in, inverse_in = normed_all[2 * ROWS :], inverse_all[2 * ROWS :]
    input_grad = grad_resid + norm_back(normed_in, inverse_in, grad_in * gains[0:1], DM)
    grad_top = input_grad.astype(BF)
    grad_rest = (input_grad - grad_top.astype(F32)).astype(BF)
    input_grad = dot(grad_top, spread, 1, 1) + dot(grad_rest, spread, 1, 1)

    other = lax.ppermute(lax.dynamic_slice_in_dim(total, (1 - core) * OWN, OWN, 0), "core", swap)
    outs = [(OWN, 256), (OWN, 256), (OWN, 512), (OWN, 512), (OWN, 512), (OWN, 256), (OWN, 256)]
    outs += [(1, OWN)] * 4 + [(1, 8)] * 2
    grad_wq, grad_wo, grad_wg, grad_wu, grad_wd, grad_wk, grad_wv, *grad_gains = call(
        final_kernel, [(shape, F32) for shape in outs], [total, other], word=core_word, vmem=16
    )
    grad_gains = [grad[0] for grad in grad_gains]
    return (
        layer_out,
        input_grad,
        grad_gains[0],
        grad_wq[:, None, :],
        grad_wk,
        grad_wv,
        grad_gains[4],
        grad_gains[5],
        grad_wo[:, None, :],
        grad_gains[1],
        grad_gains[2],
        grad_wg,
        grad_wu,
        grad_wd,
        grad_gains[3],
    )


def solution(mesh):
    fine = Mesh(mesh.devices.reshape(ZS, YS, CS, XS), EVERY)
    dp = ("z", "y", "core")
    in_specs = (
        P(EVERY, None),
        P(EVERY, None),
        P(dp),
        P(dp),
        P(dp, "x", None),
        P(dp, None),
        P(dp, None),
        P(dp),
        P(dp),
        P(dp, "x", None),
        P(dp),
        P(dp),
        P(dp, "x"),
        P(dp, "x"),
        P(dp, "x"),
        P(dp),
    )
    out_specs = (
        P(EVERY, None),
        P(EVERY, None),
        P(dp),
        P(dp, "x", None),
        P(dp, None),
        P(dp, None),
        P(dp),
        P(dp),
        P(dp, "x", None),
        P(dp),
        P(dp),
        P(dp, "x"),
        P(dp, "x"),
        P(dp, "x"),
        P(dp),
    )
    return jax.shard_map(
        per_device, mesh=fine, in_specs=in_specs, out_specs=out_specs, check_vma=False
    )
```

```python
import jax
import jax.numpy as jnp
from jax import lax
from jax.experimental import pallas as pl
from jax.experimental.pallas import tpu as pltpu
from jax.sharding import Mesh, PartitionSpec as P

WINDOW = 512
EPS = 1e-06
ROPE_BASE = 10000.0
NEGATIVE = -1e30
ZS, YS, CS, XS = 4, 4, 2, 4
CHIP = ("z", "y", "x")
EVERY = ("z", "y", "core", "x")
DPS = 32
OWN = 20
PAD = 24
DM = 640
DP = DPS * PAD
ROWS = 256
KEYS = 3 * ROWS
HQ = 4
HD = 256
HALF = HD // 2
ATT = 768
FFC = 1536
SCALE = HD**-0.5
GELU_C = 0.7978845608028654
GELU_A = 0.044715
BF = jnp.bfloat16
F32 = jnp.float32


def norm_of(values_in, width):
    inverse = lax.rsqrt(
        jnp.sum(values_in * values_in, axis=-1, keepdims=True) * (1.0 / width) + EPS
    )
    return values_in * inverse, inverse


def norm_back(normed, inverse, upstream, width):
    mean = jnp.sum(upstream * normed, axis=-1, keepdims=True) * (1.0 / width)
    return inverse * (upstream - normed * mean)


def rotate(values_in, cosine, sine):
    first, second = values_in[:, :HALF], values_in[:, HALF:]
    return jnp.concatenate(
        [first * cosine - second * sine, second * cosine + first * sine], axis=1
    )


def dot(lhs, rhs, lhs_dim, rhs_dim):
    return lax.dot_general(
        lhs, rhs, (((lhs_dim,), (rhs_dim,)), ((), ())), preferred_element_type=F32
    )


def spread_matrix():
    row = lax.broadcasted_iota(jnp.int32, (DM, DP), 0)
    col = lax.broadcasted_iota(jnp.int32, (DM, DP), 1)
    return ((col % PAD < OWN) & (row == (col // PAD) * OWN + col % PAD)).astype(BF)


def head_matrix(step):
    row = lax.broadcasted_iota(jnp.int32, (DPS * step, HD), 0)
    col = lax.broadcasted_iota(jnp.int32, (DPS * step, HD), 1)
    return ((row // step == col // 8) & (row % step == col % 8)).astype(BF)


def fetch(gathered, held, sems, first, size):
    copies = [
        pltpu.make_async_copy(gathered.at[:, x, :, first : first + size], held.at[x], sems.at[x])
        for x in range(XS)
    ]
    for copy in copies:
        copy.start()
    return copies


def cut(held, x, first, size):
    return held[x, :, :, first : first + size].reshape(DP, size)


def kv_weights(watt):
    return jnp.concatenate([cut(watt, x, 512, 128) for x in range(XS)], axis=1)


def pack_kernel(wqo_ref, wg_ref, wu_ref, wd_ref, wk_ref, wv_ref, gains_ref, at_ref, out):
    out[...] = jnp.zeros(out.shape, BF)
    out[0:OWN, 0:512] = wqo_ref[...]
    at = at_ref[0]
    kv = jnp.where(
        jnp.broadcast_to(at, (OWN, 256)) < 2, wk_ref[...].astype(F32), wv_ref[...].astype(F32)
    )
    kv = jnp.where(jnp.broadcast_to(at % 2, (OWN, 128)) == 0, kv[:, :128], kv[:, 128:])
    out[0:OWN, 512:640] = kv.astype(BF)
    out[:, 640:648] = gains_ref[...].T[:PAD].astype(BF)
    out[0:OWN, 768:1280] = wg_ref[...]
    out[0:OWN, 1280:1792] = wu_ref[...]
    out[0:OWN, 1792:2304] = wd_ref[...]


def forward_kernel(
    core_ref, gathered, normed_ref, cosine_ref, sine_ref, bias_ref, heads_ref, resid_ref, up_ref,
    spread_ref,
    gains_out, qraw_out, kvraw_out, q_out, k_out, v_out, probs_out, mixed_out,
    layer_out, dres_out, dattn_out, away_out, sums_out, z_s, dg_s, du_s, rows_t_out, ff_t_out,
    attn_t_out, gate_s, upp_s, watt, sems, wff, ff_sems,
):
    attend_copies = fetch(gathered, watt, sems, 0, ATT)
    copies = fetch(gathered, wff, ff_sems, ATT, FFC)
    for copy in attend_copies:
        copy.wait()
    gains = cut(watt, 0, 640, 128).astype(F32).T
    gains_out[0:8] = gains[0:8]
    head_gains = dot(gains.astype(BF), heads_ref[...], 1, 0)
    gains_out[8:16] = jnp.concatenate([head_gains[0:8]] * 3, axis=1)
    query_gains, key_gains = head_gains[4:5], head_gains[5:6]
    rows = (normed_ref[...] * gains[0:1]).astype(BF)
    kv_raw = dot(rows, kv_weights(watt), 1, 0)
    kvraw_out[...] = kv_raw[:, :HD]
    key_norm, _ = norm_of(kv_raw[:, :HD], HD)
    key = rotate(key_norm * key_gains, cosine_ref[...], sine_ref[...]).astype(BF)
    value = kv_raw[:, HD:].astype(BF)
    k_out[...] = key
    v_out[...] = value
    rows_own = rows[2 * ROWS :]
    cosine, sine = cosine_ref[2 * ROWS :], sine_ref[2 * ROWS :]
    attn = jnp.zeros((ROWS, DP), F32)
    for head in range(HQ):
        at = slice(head * HD, (head + 1) * HD)
        query_raw = dot(rows_own, cut(watt, head, 0, 256), 1, 0)
        qraw_out[:, at] = query_raw
        query_norm, _ = norm_of(query_raw, HD)
        query = rotate(query_norm * query_gains, cosine, sine).astype(BF)
        q_out[:, at] = query
        scores = dot(query, key, 1, 1) * SCALE + bias_ref[...]
        exponent = jnp.exp(scores - jnp.max(scores, axis=-1, keepdims=True))
        probs = exponent * (1.0 / jnp.sum(exponent, axis=-1, keepdims=True))
        probs = probs.astype(BF)
        probs_out[head] = probs
        mixed = dot(probs, value, 1, 0).astype(BF)
        mixed_out[:, at] = mixed
        attn = attn + dot(mixed, cut(watt, head, 256, 256), 1, 1)
    attn_gains, ffin_gains, ffout_gains = gains[1:2], gains[2:3], gains[3:4]
    spread = spread_ref[...]
    upstream = up_ref[...]
    attn_normed, attn_inv = norm_of(attn, DM)
    mid = resid_ref[...] + attn_normed * attn_gains
    mid_normed, mid_inv = norm_of(mid, DM)
    rows = (mid_normed * ffin_gains).astype(BF)
    ff_sum = jnp.zeros((ROWS, DP), F32)
    for x in range(XS):
        at = slice(x * 512, (x + 1) * 512)
        copies[x].wait()
        gate = dot(rows, cut(wff, x, 0, 512), 1, 0)
        up = dot(rows, cut(wff, x, 512, 512), 1, 0)
        gate_s[:, at] = gate
        upp_s[:, at] = up
        act = 0.5 * gate * (1.0 + jnp.tanh(GELU_C * (gate + GELU_A * gate * gate * gate)))
        hidden = (act * up).astype(BF)
        z_s[:, at] = hidden
        ff_sum = ff_sum + dot(hidden, cut(wff, x, 1024, 512), 1, 1)
    ff_normed, ff_inv = norm_of(ff_sum, DM)
    layer = (mid + ff_normed * ffout_gains).astype(BF)
    layer_out[...] = dot(layer, spread, 1, 1).astype(BF)
    grad_gout = jnp.sum(upstream * ff_normed, axis=0, keepdims=True)
    grad_ff = norm_back(ff_normed, ff_inv, upstream * ffout_gains, DM).astype(BF)
    grad_mid = jnp.zeros((ROWS, DP), F32)
    for x in range(XS):
        at = slice(x * 512, (x + 1) * 512)
        grad_hidden = dot(grad_ff, cut(wff, x, 1024, 512), 1, 0)
        gate, up = gate_s[:, at], upp_s[:, at]
        curve = jnp.tanh(GELU_C * (gate + GELU_A * gate * gate * gate))
        slope = 0.5 * (1.0 + curve) + 0.5 * gate * (1.0 - curve * curve) * (
            GELU_C * (1.0 + 3.0 * GELU_A * gate * gate)
        )
        grad_gate = (grad_hidden * up * slope).astype(BF)
        grad_up = (grad_hidden * (0.5 * gate * (1.0 + curve))).astype(BF)
        dg_s[:, at] = grad_gate
        du_s[:, at] = grad_up
        grad_mid = grad_mid + dot(grad_gate, cut(wff, x, 0, 512), 1, 1)
        grad_mid = grad_mid + dot(grad_up, cut(wff, x, 512, 512), 1, 1)
    grad_gfin = jnp.sum(grad_mid * mid_normed, axis=0, keepdims=True)
    grad_resid = upstream + norm_back(mid_normed, mid_inv, grad_mid * ffin_gains, DM)
    dres_out[...] = grad_resid
    grad_gattn = jnp.sum(grad_resid * attn_normed, axis=0, keepdims=True)
    dattn_out[...] = norm_back(attn_normed, attn_inv, grad_resid * attn_gains, DM).astype(BF)
    zero = jnp.zeros((1, DP), F32)
    sums_out[...] = jnp.concatenate(
        [zero, grad_gattn, grad_gfin, grad_gout, zero, zero, zero, zero], axis=0
    )
    rows_t = dot(spread, rows, 1, 1).astype(BF)
    ff_t = dot(spread, grad_ff, 1, 1).astype(BF)
    attn_t = dot(spread, dattn_out[...], 1, 1).astype(BF)
    rows_t_out[...] = rows_t
    ff_t_out[...] = ff_t
    attn_t_out[...] = attn_t
    feed_half(1 - core_ref[0], away_out, rows_t, ff_t, attn_t, z_s, dg_s, du_s, mixed_out)


def feed_half(half, out, rows_t, ff_t, attn_t, z_ref, dg_ref, du_ref, mixed_ref):
    for x in range(XS):
        cols = pl.ds(pl.multiple_of(x * 512 + half * 256, 256), 256)
        for part, (lhs, rhs) in enumerate(((rows_t, dg_ref), (rows_t, du_ref), (ff_t, z_ref))):
            grad = dot(lhs, rhs[:, cols], 1, 0).astype(BF)
            out[x, :, part * 256 : (part + 1) * 256] = grad
        cols = pl.ds(pl.multiple_of(x * 256 + half * 128, 128), 128)
        out[x, :, 768:896] = dot(attn_t, mixed_ref[:, cols], 1, 0).astype(BF)


def feed_keep_kernel(
    core_ref, z_ref, dg_ref, du_ref, rows_t_ref, ff_t_ref, attn_t_ref, mixed_ref, keep_out
):
    feed_half(
        core_ref[0], keep_out, rows_t_ref[...], ff_t_ref[...], attn_t_ref[...],
        z_ref, dg_ref, du_ref, mixed_ref,
    )


def attend_back_kernel(
    core_ref, gathered, dattn_ref, normed_ref, qraw_ref, kvraw_ref, q_ref, k_ref, v_ref,
    probs_ref, cosine_ref, sine_ref, gains_ref, sums_ref, spread_ref, heads_ref,
    keep_out, away_out, dkv2_out, dkv1_out, dkv_out, part_out, wq_s, wkv_s, watt, sems,
):
    copies = fetch(gathered, watt, sems, 0, ATT)
    spread = spread_ref[...]
    query_gains, key_gains = gains_ref[12:13, :HD], gains_ref[13:14, :HD]
    grad_attn = dattn_ref[...]
    rows = (normed_ref[...] * gains_ref[0:1]).astype(BF)
    rows_t = dot(spread, rows, 1, 1).astype(BF)
    rows_own_t = rows_t[:, 2 * ROWS :]
    key, value = k_ref[...], v_ref[...]
    cosine, sine = cosine_ref[2 * ROWS :], sine_ref[2 * ROWS :]
    for copy in copies:
        copy.wait()
    grad_key = jnp.zeros((KEYS, HD), F32)
    grad_value = jnp.zeros((KEYS, HD), F32)
    part = jnp.zeros((ROWS, DP), F32)
    grad_gq = jnp.zeros((1, HD), F32)
    for head in range(HQ):
        at = slice(head * HD, (head + 1) * HD)
        grad_mixed = dot(grad_attn, cut(watt, head, 256, 256), 1, 0).astype(BF)
        probs_low = probs_ref[head]
        probs = probs_low.astype(F32)
        grad_value = grad_value + dot(probs_low, grad_mixed, 0, 0)
        grad_probs = dot(grad_mixed, value, 1, 1)
        grad_scores = (
            probs * (grad_probs - jnp.sum(probs * grad_probs, axis=-1, keepdims=True))
        ).astype(BF)
        grad_query = dot(grad_scores, key, 1, 0) * SCALE
        grad_key = grad_key + dot(grad_scores, q_ref[:, at], 0, 0)
        query_norm, query_inv = norm_of(qraw_ref[:, at], HD)
        grad_query = rotate(grad_query, cosine, -sine)
        grad_gq = grad_gq + jnp.sum(grad_query * query_norm, axis=0, keepdims=True)
        grad_raw = norm_back(query_norm, query_inv, grad_query * query_gains, HD).astype(BF)
        part = part + dot(grad_raw, cut(watt, head, 0, 256), 1, 1)
        wq_s[:, at] = dot(rows_own_t, grad_raw, 1, 0).astype(BF)
    part_out[...] = part
    key_norm, key_inv = norm_of(kvraw_ref[...], HD)
    grad_key = rotate(grad_key * SCALE, cosine_ref[...], -sine_ref[...])
    grad_gk = jnp.sum(grad_key * key_norm, axis=0, keepdims=True)
    grad_key = norm_back(key_norm, key_inv, grad_key * key_gains, HD)
    grad_kv = jnp.concatenate([grad_key, grad_value], axis=1).astype(BF)
    dkv2_out[...] = grad_kv[:ROWS]
    dkv1_out[...] = grad_kv[ROWS : 2 * ROWS]
    dkv_out[...] = grad_kv[2 * ROWS :]
    wkv_s[...] = dot(rows_t, grad_kv, 1, 0).astype(BF)
    kv_part = dot(grad_kv, kv_weights(watt), 1, 1)
    grad_gin = jnp.sum(kv_part * normed_ref[...], axis=0, keepdims=True)
    grad_gin = grad_gin + jnp.sum(part * normed_ref[2 * ROWS :], axis=0, keepdims=True)
    model = jnp.concatenate([grad_gin, sums_ref[1:8], jnp.zeros((120, DP), F32)], axis=0)
    zeros = jnp.zeros((1, HD), F32)
    heads = jnp.concatenate(
        [zeros, zeros, zeros, zeros, grad_gq, grad_gk, zeros, zeros, jnp.zeros((120, HD), F32)],
        axis=0,
    )
    gains = dot(spread, model.astype(BF), 1, 1) + dot(heads_ref[...], heads.astype(BF), 1, 1)
    gains = gains.astype(BF)
    core = core_ref[0]
    own_kv = jnp.broadcast_to(core, (DM, 128)) == 0
    for x in range(XS):
        for out, half in ((keep_out, core), (away_out, 1 - core)):
            cols = pl.ds(pl.multiple_of(x * 256 + half * 128, 128), 128)
            out[:, x, :, 0:128] = wq_s[:, cols].astype(F32).reshape(16, 40, 128).astype(BF)
        kv = wkv_s[:, x * 128 : (x + 1) * 128].astype(F32)
        kept = jnp.where(own_kv, kv, gains.astype(F32)).reshape(16, 40, 128).astype(BF)
        sent = jnp.where(own_kv, gains.astype(F32), kv).reshape(16, 40, 128).astype(BF)
        keep_out[:, x, :, 128:256] = kept
        away_out[:, x, :, 128:256] = sent


def final_kernel(core_ref, total_ref, other_ref, wq, wo, wg, wu, wd, wk, wv, *gain_refs):
    first = jnp.broadcast_to(core_ref[0], (OWN, total_ref.shape[1])) == 0
    mine = jnp.where(first, total_ref[0:OWN], total_ref[OWN : 2 * OWN])
    other = other_ref[...]
    left = jnp.where(first, mine, other)
    right = jnp.where(first, other, mine)
    for ref, at, size in ((wg, 0, 256), (wu, 256, 256), (wd, 512, 256), (wo, 768, 128), (wq, 896, 128)):
        ref[:, :size] = left[:, at : at + size]
        ref[:, size:] = right[:, at : at + size]
    wk[...] = left[:, 1152:1408]
    wv[...] = left[:, 1408:1664]
    gains = jnp.concatenate([right[:, 1024:1152], jnp.zeros((PAD - OWN, 128), F32)], axis=0).T
    for row, ref in enumerate(gain_refs):
        ref[...] = gains[row : row + 1, : ref.shape[1]]


def call(kernel, outs, args, scratch=(), word=None, weights=None, flops=0, vmem=0):
    whole = pl.BlockSpec(memory_space=pltpu.VMEM)
    first, first_specs = [], []
    if word is not None:
        first, first_specs = [word], [pl.BlockSpec(memory_space=pltpu.SMEM)]
    shapes = [pltpu.VMEM(shape, kind) for shape, kind in scratch]
    if weights is not None:
        gathered, *sizes = weights
        first, first_specs = first + [gathered], first_specs + [pl.BlockSpec(memory_space=pl.ANY)]
        for size in sizes:
            shapes += [pltpu.VMEM((XS, DPS, PAD, size), BF), pltpu.SemaphoreType.DMA((XS,))]
    return pl.pallas_call(
        kernel,
        out_shape=[jax.ShapeDtypeStruct(shape, kind) for shape, kind in outs],
        in_specs=first_specs + [whole] * len(args),
        out_specs=[whole] * len(outs),
        scratch_shapes=shapes,
        compiler_params=pltpu.CompilerParams(vmem_limit_bytes=vmem * 2**20),
        cost_estimate=pl.CostEstimate(flops=flops, bytes_accessed=20 * 2**20, transcendentals=0),
    )(*first, *args)


def per_device(
    hidden_in,
    out_grad,
    segment_ids,
    gain_input,
    w_query,
    w_key,
    w_value,
    gain_query,
    gain_key,
    w_out,
    gain_attn,
    gain_ffin,
    w_gate,
    w_up,
    w_down,
    gain_ffout,
):
    at = lax.axis_index("x")
    core = lax.axis_index("core")

    gains_own = jnp.zeros((8, 128), F32)
    for row, gain in enumerate(
        (gain_input, gain_attn, gain_ffin, gain_ffout, gain_query, gain_key)
    ):
        size = gain.shape[0]
        gains_own = gains_own + jnp.pad(
            gain.astype(F32)[None], ((row, 7 - row), (0, 128 - size))
        )
    width = ATT + FFC
    at_word = at.astype(jnp.int32).reshape(1)
    whole = pl.BlockSpec(memory_space=pltpu.VMEM)
    packed = pl.pallas_call(
        pack_kernel,
        out_shape=jax.ShapeDtypeStruct((PAD, width), BF),
        in_specs=[whole] * 7 + [pl.BlockSpec(memory_space=pltpu.SMEM)],
        out_specs=whole,
    )(jnp.concatenate([w_query[:, 0], w_out[:, 0]], axis=1), w_gate, w_up, w_down, w_key, w_value, gains_own, at_word)
    gathered = lax.all_gather(packed, EVERY, axis=0, tiled=False).reshape(DPS, XS, PAD, width)

    before_one = lax.ppermute(hidden_in, "x", [(i, i + 1) for i in range(XS - 1)])
    before_two = lax.ppermute(hidden_in, "x", [(i, i + 2) for i in range(XS - 2)])
    rows_low = jnp.concatenate([before_two, before_one, hidden_in], axis=0)
    spread = spread_matrix()
    resid_all = dot(rows_low, spread, 1, 0)
    upstream = dot(out_grad, spread, 1, 0)
    normed_all, inverse_all = norm_of(resid_all, DM)
    resid_in = resid_all[2 * ROWS :]

    offsets = jnp.arange(segment_ids.shape[0], dtype=jnp.int32)
    live = segment_ids >= 0
    tail_start = jnp.sum(live.astype(jnp.int32))
    positions = offsets - jnp.where(live, segment_ids, tail_start)
    positions = jnp.concatenate([jnp.zeros((2 * ROWS,), jnp.int32), positions], axis=0)
    positions = lax.dynamic_slice_in_dim(positions, at * ROWS, KEYS, 0)
    frequency = ROPE_BASE ** (-2.0 * jnp.arange(HALF, dtype=F32) / HD)
    angles = positions.astype(F32)[:, None] * frequency[None, :]
    cosine, sine = jnp.cos(angles), jnp.sin(angles)
    ids = jnp.concatenate([jnp.full((2 * ROWS,), -2, jnp.int32), segment_ids], axis=0)
    key_ids = lax.dynamic_slice_in_dim(ids, at * ROWS, KEYS, 0)
    query_ids = key_ids[2 * ROWS :]
    row_at = lax.broadcasted_iota(jnp.int32, (ROWS, KEYS), 0)
    col_at = lax.broadcasted_iota(jnp.int32, (ROWS, KEYS), 1)
    gap = row_at + 2 * ROWS - col_at
    visible = (
        (query_ids[:, None] == key_ids[None, :])
        & (gap >= 0)
        & (gap < WINDOW)
        & ((query_ids[:, None] >= 0) | (gap == 0))
    )
    bias = jnp.where(visible, 0.0, NEGATIVE).astype(F32)

    core_word = core.astype(jnp.int32).reshape(1)
    head_rows = head_matrix(OWN)
    core_word, head_rows = lax.optimization_barrier((core_word, head_rows))
    (
        gains, query_raw, kv_raw, query, key, value, probs, mixed,
        layer_out, grad_resid, grad_attn, away_ff, sums, *feed,
    ) = call(
        forward_kernel,
        [
            ((16, DP), F32),
            ((ROWS, HQ * HD), F32),
            ((KEYS, HD), F32),
            ((ROWS, HQ * HD), BF),
            ((KEYS, HD), BF),
            ((KEYS, HD), BF),
            ((HQ, ROWS, KEYS), BF),
            ((ROWS, HQ * HD), BF),
            ((ROWS, DM), BF),
            ((ROWS, DP), F32),
            ((ROWS, DP), BF),
            ((XS, DM, 896), BF),
            ((8, DP), F32),
            ((ROWS, 2048), BF),
            ((ROWS, 2048), BF),
            ((ROWS, 2048), BF),
            ((DM, ROWS), BF),
            ((DM, ROWS), BF),
            ((DM, ROWS), BF),
        ],
        [normed_all, cosine, sine, bias, head_matrix(PAD), resid_in, upstream, spread],
        [((ROWS, 2048), F32), ((ROWS, 2048), F32)],
        word=core_word,
        weights=(gathered, ATT, FFC),
        flops=10**10,
        vmem=50,
    )
    swap = [(0, 1), (1, 0)]
    arrived_ff = lax.ppermute(away_ff, "core", swap)
    (keep_ff,) = call(
        feed_keep_kernel, [((XS, DM, 896), BF)], feed + [mixed], word=core_word, flops=2 * 10**9, vmem=20
    )
    both_ff = (keep_ff.astype(F32) + arrived_ff.astype(F32)).astype(BF)
    both_ff, grad_attn = lax.optimization_barrier((both_ff, grad_attn))
    column_ff = lax.psum_scatter(
        both_ff.reshape(XS * DM, 896), "x", scatter_dimension=0, tiled=True
    )
    keep_att, away_att, grad_kv_two, grad_kv_one, grad_kv, query_part = call(
        attend_back_kernel,
        [
            ((16, XS, 40, 256), BF),
            ((16, XS, 40, 256), BF),
            ((ROWS, 2 * HD), BF),
            ((ROWS, 2 * HD), BF),
            ((ROWS, 2 * HD), BF),
            ((ROWS, DP), F32),
        ],
        [
            grad_attn, normed_all, query_raw, kv_raw, query, key, value, probs,
            cosine, sine, gains, sums, spread, head_rows,
        ],
        [((DM, 1024), BF), ((DM, 512), BF)],
        word=core_word,
        weights=(gathered, ATT),
        flops=4 * 10**9,
        vmem=60,
    )
    arrived_att = lax.ppermute(away_att, "core", swap)
    from_one = lax.ppermute(
        grad_kv_one, "x", [(i + 1, i) for i in range(XS - 1)]
    )
    from_two = lax.ppermute(grad_kv_two, "x", [(i + 2, i) for i in range(XS - 2)])
    both_att = (keep_att.astype(F32) + arrived_att.astype(F32)).astype(BF)
    parts_att = lax.all_to_all(both_att.reshape(16, 160, 256), ("z", "y"), 0, 0, tiled=True)
    parts_att, column_ff = lax.optimization_barrier((parts_att, column_ff))
    row_att = jnp.sum(parts_att.astype(F32), axis=0).astype(BF)
    one, two, three = (
        lax.ppermute(row_att, "x", [(i, (i + step) % XS) for i in range(XS)]).astype(F32)
        for step in (1, 2, 3)
    )
    all_att = ((row_att.astype(F32) + two) + (one + three)).reshape(XS, 40, 256)
    total_att = lax.dynamic_index_in_dim(all_att, at, 0, keepdims=False)
    total_kv = all_att[:, :, 128:].transpose(1, 0, 2).reshape(40, 512)
    parts_ff = lax.all_to_all(column_ff.reshape(16, 40, 896), ("z", "y"), 0, 0, tiled=True)
    total_ff = jnp.sum(parts_ff.astype(F32), axis=0)
    total = jnp.concatenate([total_ff, total_att, total_kv], axis=1)

    grad_kv_own = (
        grad_kv.astype(F32) + from_one.astype(F32) + from_two.astype(F32)
    ).astype(BF)
    kv_cols = gathered[:, :, :, 512:640].transpose(0, 2, 1, 3).reshape(DP, 2 * HD)
    grad_in = query_part + dot(grad_kv_own, kv_cols, 1, 1)
    normed_in, inverse_in = normed_all[2 * ROWS :], inverse_all[2 * ROWS :]
    input_grad = grad_resid + norm_back(normed_in, inverse_in, grad_in * gains[0:1], DM)
    grad_top = input_grad.astype(BF)
    grad_rest = (input_grad - grad_top.astype(F32)).astype(BF)
    input_grad = dot(grad_top, spread, 1, 1) + dot(grad_rest, spread, 1, 1)

    other = lax.ppermute(lax.dynamic_slice_in_dim(total, (1 - core) * OWN, OWN, 0), "core", swap)
    outs = [(OWN, 256), (OWN, 256), (OWN, 512), (OWN, 512), (OWN, 512), (OWN, 256), (OWN, 256)]
    outs += [(1, OWN)] * 4 + [(1, 8)] * 2
    grad_wq, grad_wo, grad_wg, grad_wu, grad_wd, grad_wk, grad_wv, *grad_gains = call(
        final_kernel, [(shape, F32) for shape in outs], [total, other], word=core_word, vmem=16
    )
    grad_gains = [grad[0] for grad in grad_gains]
    return (
        layer_out,
        input_grad,
        grad_gains[0],
        grad_wq[:, None, :],
        grad_wk,
        grad_wv,
        grad_gains[4],
        grad_gains[5],
        grad_wo[:, None, :],
        grad_gains[1],
        grad_gains[2],
        grad_wg,
        grad_wu,
        grad_wd,
        grad_gains[3],
    )


def solution(mesh):
    fine = Mesh(mesh.devices.reshape(ZS, YS, CS, XS), EVERY)
    dp = ("z", "y", "core")
    in_specs = (
        P(EVERY, None),
        P(EVERY, None),
        P(dp),
        P(dp),
        P(dp, "x", None),
        P(dp, None),
        P(dp, None),
        P(dp),
        P(dp),
        P(dp, "x", None),
        P(dp),
        P(dp),
        P(dp, "x"),
        P(dp, "x"),
        P(dp, "x"),
        P(dp),
    )
    out_specs = (
        P(EVERY, None),
        P(EVERY, None),
        P(dp),
        P(dp, "x", None),
        P(dp, None),
        P(dp, None),
        P(dp),
        P(dp),
        P(dp, "x", None),
        P(dp),
        P(dp),
        P(dp, "x"),
        P(dp, "x"),
        P(dp, "x"),
        P(dp),
    )
    return jax.shard_map(
        per_device, mesh=fine, in_specs=in_specs, out_specs=out_specs, check_vma=False
    )
```
